32 devices in a mesh: lon: 4 (over x, core), lat: 8 (over z, y).
Axes of the slice: x: 2, y: 2, z: 4, core: 2. Of those that a mesh axis runs over, the one named last changes fastest.
Arguments:
- model_state: float32 [4, 8, 256, 5760], P(None, None, 'lat', 'lon')
- courant: float32 [256], P('lat'), may hold values from 0.02 to 0.08
- cutoff: int32 [256], replicated, may hold values from 1 to 2880, as said below
Outputs:
- new_state: float32 [4, 8, 256, 5760], P(None, None, 'lat', 'lon')
The draws below stay inside these ranges and needn't reach their ends.
Inputs may be any that keep to these rules, and one draw needn't show every extreme that they name: `cutoff`: rows 64 to 191 hold 5760/2 (no damping); every other row holds less.
All inputs are finite; a program needn't handle non-finite values.
Results may differ from the reference program's by a relative error of at most 0.000073.
Values sent between devices are 32-bit elements; how exact they have to be, the bound alone decides.
A program may use at most 64 MiB of HBM per device.

```python
import math
import jax
import jax.numpy as jnp
from jax import lax

NLON = 5760
LEV = 8
NLAT = 256


def draw_model_state(key, part):
    key_list = jax.random.split(jax.random.fold_in(key, 11), 4)
    field_shape = (LEV, NLAT, NLON)
    wind_east = jax.random.truncated_normal(key_list[0], -3.0, 3.0, field_shape, jnp.float32)
    wind_north = jax.random.truncated_normal(key_list[1], -3.0, 3.0, field_shape, jnp.float32)
    theta = jnp.exp(jax.random.uniform(key_list[2], field_shape, jnp.float32, math.log(0.5), math.log(2.0)))
    thickness = jax.random.uniform(key_list[3], field_shape, jnp.float32, 2.0, 3.0)
    return jnp.stack([wind_east, wind_north, theta, thickness]).astype(jnp.float32)


def draw_cutoff(key, part):
    row_index = jnp.arange(NLAT, dtype=jnp.int32)
    quarter = NLAT // 4
    distance = jnp.where(row_index < quarter, row_index, NLAT - 1 - row_index)
    base_cut = NLON // 2 * (2 * distance + 1) // (2 * quarter)
    jitter = jax.random.randint(jax.random.fold_in(key, 23), (NLAT,), 0, 1048576) % (base_cut // 4 + 1)
    polar_cut = jnp.maximum(1, base_cut - jitter)
    is_polar = (row_index < quarter) | (row_index >= NLAT - quarter)
    return jnp.where(is_polar, polar_cut, NLON // 2).astype(jnp.int32)


def shard_levels(key, extent, shards, low, largest):
    factor_of, own = 1.0, jax.random.fold_in(key, 6)
    for position, parts in shards:
        draws = jnp.exp(jax.random.uniform(jax.random.fold_in(own, position), (parts,), jnp.float32, low / len(shards), largest / len(shards)))
        factor_of = factor_of * jnp.repeat(draws, extent[position] // parts).reshape([-1 if axis == position else 1 for axis in range(len(extent))])
    return factor_of


def setup_inputs(seed: int = 0) -> dict:
    arg_keys = jax.random.split(jax.random.key(seed), 4)
    return {
        "model_state": draw_model_state(jax.random.fold_in(arg_keys[3], 71), 0),
        "courant": jnp.clip(jnp.exp(math.log(0.08) - 1.3862944 * jax.random.uniform(arg_keys[1], (NLAT,), jnp.float32) ** shard_levels(arg_keys[1], (NLAT,), ((0, 8),), -0.2, 0.2)), 0.02, 0.08),
        "cutoff": draw_cutoff(jax.random.fold_in(arg_keys[3], 71), 0),
    }


meridional_courant = 0.05
pressure_gain = 4.0


def along_lon(field):
    return (jnp.roll(field, -1, axis=-1) - jnp.roll(field, 1, axis=-1)) * 0.5


def along_lat(field):
    padded = jnp.pad(field, ((0, 0), (1, 1), (0, 0)))
    return (padded[:, 2:, :] - padded[:, :-2, :]) * 0.5


def reference(model_state, courant, cutoff):
    wind_east = model_state[0]
    wind_north = model_state[1]
    theta = model_state[2]
    thickness = model_state[3]
    row_courant = courant[None, :, None]
    east_flux = wind_east * thickness
    north_flux = wind_north * thickness
    new_thickness = thickness - row_courant * along_lon(east_flux) - meridional_courant * along_lat(north_flux)
    heat_content = theta * thickness
    new_heat = heat_content - row_courant * along_lon(east_flux * theta) - meridional_courant * along_lat(north_flux * theta)
    new_theta = new_heat / new_thickness
    new_east = wind_east - pressure_gain * row_courant * along_lon(new_heat)
    new_north = wind_north - pressure_gain * meridional_courant * along_lat(new_heat)
    stacked = jnp.stack([new_east, new_north, new_theta, new_thickness])
    wave_number = jnp.arange(NLON, dtype=jnp.int32)
    folded = jnp.minimum(wave_number, NLON - wave_number)
    cut_ratio = cutoff.astype(jnp.float32)[:, None] / jnp.maximum(folded, 1).astype(jnp.float32)[None, :]
    damping = jnp.minimum(1.0, cut_ratio * cut_ratio)

    def filter_field(field):
        spectrum = jnp.fft.fft(field, axis=-1)
        return jnp.real(jnp.fft.ifft(spectrum * damping[None], axis=-1))

    filtered = lax.map(filter_field, stacked)
    return filtered.astype(jnp.float32)
```

```python
import jax
import jax.numpy as jnp
import numpy as np
from jax import lax
from jax.sharding import PartitionSpec as P

meridional_courant = 0.05
pressure_gain = 4.0


def with_halo(array, sides, width):
    for axis, dim in sides:
        size, length = (lax.axis_size(axis), array.shape[dim])
        up = [(i, (i + 1) % size) for i in range(size)]
        down = [(j, i) for i, j in up]
        last = lax.slice_in_dim(array, length - width, length, axis=dim)
        first = lax.slice_in_dim(array, 0, width, axis=dim)
        before = lax.ppermute(last, axis, up)
        after = lax.ppermute(first, axis, down)
        array = jnp.concatenate([before, array, after], axis=dim)
    return array


def quarter_basis(quarter):
    half = quarter // 2
    lanes = -(-(half + 1) // 128) * 128
    phase = np.outer(np.arange(quarter), np.arange(half + 1)) % quarter
    angle = 2.0 * np.pi / quarter * phase
    table = np.zeros((quarter, 2 * lanes), np.float32)
    table[:, : half + 1] = np.cos(angle)
    table[:, lanes : lanes + half + 1] = np.sin(angle)
    return table


def quarter_twists(quarter):
    angle = 2.0 * np.pi / (4 * quarter) * np.outer([1.0, 2.0], np.arange(quarter))
    return np.cos(angle).astype(np.float32), np.sin(angle).astype(np.float32)


def damping_tables(row_cutoff, quarter):
    half = quarter // 2
    length = 4 * quarter
    lanes = -(-(half + 1) // 128) * 128
    index = jnp.arange(lanes, dtype=jnp.int32)
    inside = index <= half
    weight = jnp.where(inside, jnp.where((index == 0) | (index == half), 1.0, 2.0), 0.0) / quarter
    cut = row_cutoff.astype(jnp.float32)[:, None]

    def damping(wave_number):
        wave_number = jnp.abs(wave_number)
        folded = jnp.minimum(wave_number, length - wave_number)
        ratio = cut / jnp.maximum(folded, 1).astype(jnp.float32)[None, :]
        return jnp.minimum(1.0, ratio * ratio)

    def pair(shift, scale):
        above = damping(4 * index + shift)
        below = damping(4 * index - shift)
        gain = weight[None, :] * (0.5 * scale)
        return gain * (above + below), gain * (above - below)

    return pair(0, 0.25)[0], pair(2, 0.25), pair(1, 0.5)


def mix(real_cos, real_sin, imag_cos, imag_sin, same, cross):
    return (
        same * real_cos + cross * imag_sin,
        same * real_sin - cross * imag_cos,
        same * imag_cos - cross * real_sin,
        same * imag_sin + cross * real_cos,
    )


def damp_quarters(quarters, row_cutoff):
    _, planes, rows, quarter = quarters.shape
    basis = jnp.asarray(quarter_basis(quarter))
    cos_twist, sin_twist = quarter_twists(quarter)
    q0, q1, q2, q3 = quarters
    even, odd_a, odd_b = (q0 + q2) + (q1 + q3), q0 - q2, q1 - q3
    skew = (q0 + q2) - (q1 + q3)
    pairs = planes // 2
    skew_a, skew_b = skew[:pairs], skew[pairs:]
    one_real = odd_a * cos_twist[0] - odd_b * sin_twist[0]
    one_imag = -odd_a * sin_twist[0] - odd_b * cos_twist[0]
    two_real = skew_a * cos_twist[1] + skew_b * sin_twist[1]
    two_imag = skew_b * cos_twist[1] - skew_a * sin_twist[1]
    stack = jnp.concatenate([even, two_real, two_imag, one_real, one_imag], axis=0)
    waves = jnp.einsum("prm,mk->prk", stack, basis, precision=lax.Precision.HIGH)
    lanes = basis.shape[1] // 2
    cos_part, sin_part = waves[..., :lanes], waves[..., lanes:]
    same0, (same2, cross2), (same1, cross1) = damping_tables(row_cutoff, quarter)
    p, h = planes, pairs
    two = slice(p, p + h), slice(p + h, 2 * p)
    one = slice(2 * p, 3 * p), slice(3 * p, 4 * p)
    even_c, even_s = same0 * cos_part[:p], same0 * sin_part[:p]
    rc2, rs2, ic2, is2 = mix(
        cos_part[two[0]], sin_part[two[0]], cos_part[two[1]], sin_part[two[1]], same2, cross2
    )
    rc1, rs1, ic1, is1 = mix(
        cos_part[one[0]], sin_part[one[0]], cos_part[one[1]], sin_part[one[1]], same1, cross1
    )
    damped = jnp.concatenate(
        [
            jnp.concatenate([even_c, rc2, ic2, rc1, ic1], axis=0),
            jnp.concatenate([even_s, rs2, is2, rs1, is1], axis=0),
        ],
        axis=-1,
    )
    back = jnp.einsum("prk,mk->prm", damped, basis, precision=lax.Precision.HIGH)
    even, two_real, two_imag = back[:p], back[two[0]], back[two[1]]
    one_real, one_imag = back[one[0]], back[one[1]]
    odd_a = one_real * cos_twist[0] - one_imag * sin_twist[0]
    odd_b = -one_real * sin_twist[0] - one_imag * cos_twist[0]
    skew = jnp.concatenate(
        [
            two_real * cos_twist[1] - two_imag * sin_twist[1],
            two_imag * cos_twist[1] + two_real * sin_twist[1],
        ],
        axis=0,
    )
    plus, minus = even + skew, even - skew
    return jnp.stack([plus + odd_a, minus + odd_b, plus - odd_a, minus - odd_b])


def trim_rims(extended, row_dim):
    band_index = lax.axis_index("lat")
    band_count = lax.axis_size("lat")
    rows_ext = extended.shape[row_dim]
    positions = jnp.arange(rows_ext, dtype=jnp.int32)
    keep_rows = jnp.logical_not(
        (positions == 0) & (band_index == 0)
        | (positions == rows_ext - 1) & (band_index == band_count - 1)
    )
    mask_shape = [1] * extended.ndim
    mask_shape[row_dim] = rows_ext
    return extended * keep_rows.astype(extended.dtype).reshape(mask_shape)


def along_lon(field_ext):
    return (field_ext[..., 1:-1, 2:] - field_ext[..., 1:-1, :-2]) * 0.5


def along_lat(field_ext):
    return (field_ext[..., 2:, 1:-1] - field_ext[..., :-2, 1:-1]) * 0.5


def filter_block(work_block, block_cutoff):
    lon_parts = lax.axis_size("lon")
    components, levels, rows_here, width_here = work_block.shape
    planes = components * levels // lon_parts
    group = lon_parts // 4
    lines = work_block.reshape(lon_parts, planes, rows_here, width_here)
    circles = lax.all_to_all(lines, "lon", split_axis=0, concat_axis=0, tiled=True)
    quarters = circles.reshape(4, group, planes, rows_here, width_here)
    quarters = jnp.moveaxis(quarters, 1, 3).reshape(4, planes, rows_here, group * width_here)
    smoothed = damp_quarters(quarters, block_cutoff)
    smoothed = smoothed.reshape(4, planes, rows_here, group, width_here)
    smoothed = jnp.moveaxis(smoothed, 3, 1).reshape(lines.shape)
    returned = lax.all_to_all(smoothed, "lon", split_axis=0, concat_axis=0, tiled=True)
    return returned.reshape(work_block.shape)


def per_device(model_state, courant, cutoff):
    rows_here = model_state.shape[2]
    band_index = lax.axis_index("lat")
    extended = with_halo(model_state, (("lon", 3), ("lat", 2)), 1)
    extended = trim_rims(extended, 2)
    wind_east = extended[0]
    wind_north = extended[1]
    theta_ext = extended[2]
    thickness = extended[3]
    row_courant = courant[None, :, None]
    east_flux = wind_east * thickness
    north_flux = wind_north * thickness
    heat_content = theta_ext * thickness
    new_thickness = (
        thickness[:, 1:-1, 1:-1]
        - row_courant * along_lon(east_flux)
        - meridional_courant * along_lat(north_flux)
    )
    new_heat = (
        heat_content[:, 1:-1, 1:-1]
        - row_courant * along_lon(east_flux * theta_ext)
        - meridional_courant * along_lat(north_flux * theta_ext)
    )
    new_theta = new_heat / new_thickness
    heat_ext = trim_rims(with_halo(new_heat, (("lon", 2), ("lat", 1)), 1), 1)
    new_east = wind_east[:, 1:-1, 1:-1] - pressure_gain * row_courant * along_lon(heat_ext)
    new_north = wind_north[:, 1:-1, 1:-1] - pressure_gain * meridional_courant * along_lat(heat_ext)
    stacked = jnp.stack([new_east, new_north, new_theta, new_thickness])
    own_cut = lax.dynamic_slice_in_dim(cutoff, band_index * rows_here, rows_here)
    return filter_block(stacked, own_cut)


def solution(mesh):
    placed = (P(None, None, "lat", "lon"), P("lat"), P())
    return jax.shard_map(
        per_device,
        mesh=mesh,
        in_specs=placed,
        out_specs=P(None, None, "lat", "lon"),
        check_vma=False,
    )
```

```python
import functools

import jax
import jax.numpy as jnp
import numpy as np
from jax import lax
from jax.experimental import pallas as pl
from jax.experimental.pallas import tpu as pltpu
from jax.sharding import PartitionSpec as P

meridional_courant = 0.05
pressure_gain = 4.0
MESH = pl.DeviceIdType.MESH


def with_halo(array, sides, width):
    for axis, dim in sides:
        size, length = (lax.axis_size(axis), array.shape[dim])
        up = [(i, (i + 1) % size) for i in range(size)]
        down = [(j, i) for i, j in up]
        last = lax.slice_in_dim(array, length - width, length, axis=dim)
        first = lax.slice_in_dim(array, 0, width, axis=dim)
        before = lax.ppermute(last, axis, up)
        after = lax.ppermute(first, axis, down)
        array = jnp.concatenate([before, array, after], axis=dim)
    return array


def quarter_basis(quarter):
    half = quarter // 2
    lanes = -(-(half + 1) // 128) * 128
    phase = np.outer(np.arange(quarter), np.arange(half + 1)) % quarter
    angle = 2.0 * np.pi / quarter * phase
    table = np.zeros((quarter, 2 * lanes), np.float32)
    table[:, : half + 1] = np.cos(angle)
    table[:, lanes : lanes + half + 1] = np.sin(angle)
    return table


def quarter_twists(quarter):
    angle = 2.0 * np.pi / (4 * quarter) * np.outer([1.0, 2.0], np.arange(quarter))
    return np.cos(angle).astype(np.float32), np.sin(angle).astype(np.float32)


def damping_tables(row_cutoff, quarter):
    half = quarter // 2
    length = 4 * quarter
    lanes = -(-(half + 1) // 128) * 128
    index = jnp.arange(lanes, dtype=jnp.int32)
    inside = index <= half
    weight = jnp.where(inside, jnp.where((index == 0) | (index == half), 1.0, 2.0), 0.0) / quarter
    cut = row_cutoff.astype(jnp.float32)[:, None]

    def damping(wave_number):
        wave_number = jnp.abs(wave_number)
        folded = jnp.minimum(wave_number, length - wave_number)
        ratio = cut / jnp.maximum(folded, 1).astype(jnp.float32)[None, :]
        return jnp.minimum(1.0, ratio * ratio)

    def pair(shift, scale):
        above = damping(4 * index + shift)
        below = damping(4 * index - shift)
        gain = weight[None, :] * (0.5 * scale)
        return gain * (above + below), gain * (above - below)

    return pair(0, 0.25)[0], pair(2, 0.25), pair(1, 0.5)


def mix(real_cos, real_sin, imag_cos, imag_sin, same, cross):
    return (
        same * real_cos + cross * imag_sin,
        same * real_sin - cross * imag_cos,
        same * imag_cos - cross * real_sin,
        same * imag_sin + cross * real_cos,
    )


def damp_quarters(quarters, row_cutoff):
    _, planes, rows, quarter = quarters.shape
    basis = jnp.asarray(quarter_basis(quarter))
    cos_twist, sin_twist = quarter_twists(quarter)
    q0, q1, q2, q3 = quarters
    even, odd_a, odd_b = (q0 + q2) + (q1 + q3), q0 - q2, q1 - q3
    skew = (q0 + q2) - (q1 + q3)
    pairs = planes // 2
    skew_a, skew_b = skew[:pairs], skew[pairs:]
    one_real = odd_a * cos_twist[0] - odd_b * sin_twist[0]
    one_imag = -odd_a * sin_twist[0] - odd_b * cos_twist[0]
    two_real = skew_a * cos_twist[1] + skew_b * sin_twist[1]
    two_imag = skew_b * cos_twist[1] - skew_a * sin_twist[1]
    stack = jnp.concatenate([even, two_real, two_imag, one_real, one_imag], axis=0)
    waves = jnp.einsum("prm,mk->prk", stack, basis, precision=lax.Precision.HIGH)
    lanes = basis.shape[1] // 2
    cos_part, sin_part = waves[..., :lanes], waves[..., lanes:]
    same0, (same2, cross2), (same1, cross1) = damping_tables(row_cutoff, quarter)
    p, h = planes, pairs
    two = slice(p, p + h), slice(p + h, 2 * p)
    one = slice(2 * p, 3 * p), slice(3 * p, 4 * p)
    even_c, even_s = same0 * cos_part[:p], same0 * sin_part[:p]
    rc2, rs2, ic2, is2 = mix(
        cos_part[two[0]], sin_part[two[0]], cos_part[two[1]], sin_part[two[1]], same2, cross2
    )
    rc1, rs1, ic1, is1 = mix(
        cos_part[one[0]], sin_part[one[0]], cos_part[one[1]], sin_part[one[1]], same1, cross1
    )
    damped = jnp.concatenate(
        [
            jnp.concatenate([even_c, rc2, ic2, rc1, ic1], axis=0),
            jnp.concatenate([even_s, rs2, is2, rs1, is1], axis=0),
        ],
        axis=-1,
    )
    back = jnp.einsum("prk,mk->prm", damped, basis, precision=lax.Precision.HIGH)
    even, two_real, two_imag = back[:p], back[two[0]], back[two[1]]
    one_real, one_imag = back[one[0]], back[one[1]]
    odd_a = one_real * cos_twist[0] - one_imag * sin_twist[0]
    odd_b = -one_real * sin_twist[0] - one_imag * cos_twist[0]
    skew = jnp.concatenate(
        [
            two_real * cos_twist[1] - two_imag * sin_twist[1],
            two_imag * cos_twist[1] + two_real * sin_twist[1],
        ],
        axis=0,
    )
    plus, minus = even + skew, even - skew
    return jnp.stack([plus + odd_a, minus + odd_b, plus - odd_a, minus - odd_b])


def trim_rims(extended, row_dim):
    band_index = lax.axis_index("lat")
    band_count = lax.axis_size("lat")
    rows_ext = extended.shape[row_dim]
    positions = jnp.arange(rows_ext, dtype=jnp.int32)
    keep_rows = jnp.logical_not(
        (positions == 0) & (band_index == 0)
        | (positions == rows_ext - 1) & (band_index == band_count - 1)
    )
    mask_shape = [1] * extended.ndim
    mask_shape[row_dim] = rows_ext
    return extended * keep_rows.astype(extended.dtype).reshape(mask_shape)


def along_lon(field_ext):
    return (field_ext[..., 1:-1, 2:] - field_ext[..., 1:-1, :-2]) * 0.5


def along_lat(field_ext):
    return (field_ext[..., 2:, 1:-1] - field_ext[..., :-2, 1:-1]) * 0.5


def filter_block(work_block, block_cutoff):
    lon_parts = lax.axis_size("lon")
    components, levels, rows_here, width_here = work_block.shape
    planes = components * levels // lon_parts
    group = lon_parts // 4
    lines = work_block.reshape(lon_parts, planes, rows_here, width_here)
    circles = lax.all_to_all(lines, "lon", split_axis=0, concat_axis=0, tiled=True)
    quarters = circles.reshape(4, group, planes, rows_here, width_here)
    quarters = jnp.moveaxis(quarters, 1, 3).reshape(4, planes, rows_here, group * width_here)
    smoothed = damp_quarters(quarters, block_cutoff)
    smoothed = smoothed.reshape(4, planes, rows_here, group, width_here)
    smoothed = jnp.moveaxis(smoothed, 3, 1).reshape(lines.shape)
    returned = lax.all_to_all(smoothed, "lon", split_axis=0, concat_axis=0, tiled=True)
    return returned.reshape(work_block.shape)


def worker_group(band, bands):
    quarter = bands // 4
    low = band < bands // 2
    polar = jnp.logical_or(band < quarter, band >= bands - quarter)
    inner = jnp.where(low, band - quarter, band + quarter)
    source = jnp.where(polar, band, inner)
    helper = jnp.where(source < bands // 2, source + quarter, source - quarter)
    return polar, source, helper


def split_store(ref, values):
    rows, width = values.shape
    high = values.astype(jnp.bfloat16)
    low = (values - high.astype(jnp.float32)).astype(jnp.bfloat16)
    ref[:rows, :width] = high
    ref[rows:, :width] = low


def product(parts, high_ref, low_ref, out_ref, back):
    rows = out_ref.shape[0]
    dims = (((1,), (1 if back else 0,)), ((), ()))
    for start in range(0, out_ref.shape[1], 256):
        cols = slice(start, start + 256)
        piece = (cols, slice(None)) if back else (slice(None), cols)
        both = lax.dot_general(parts[...], high_ref[piece], dims, preferred_element_type=jnp.float32)
        cross = lax.dot_general(
            parts[:rows, :], low_ref[piece], dims, preferred_element_type=jnp.float32
        )
        out_ref[:, cols] = (both[:rows] + both[rows:]) + cross


def circle_kernel(
    bands, parts, chunks, state, gains, twists, tables, out, circles, results, high, low, operand, waves,
    send_sem, recv_sem, back_send_sem, back_recv_sem, local_sem,
):
    part = lax.axis_index("lon")
    band = lax.axis_index("lat")
    polar, source, helper = worker_group(band, bands)
    _, _, per, rows, quarter = circles.shape
    width = high.shape[1]
    lanes = width // 2
    workers = 2 * parts
    row_chunks = state.shape[1] // rows
    planes_per = state.shape[0] // workers
    me = jnp.where(polar, part, part + parts)

    def block(ref, worker, chunk):
        plane = worker * planes_per + (chunk // row_chunks) * per
        row = pl.multiple_of((chunk % row_chunks) * rows, rows)
        return ref.at[pl.ds(plane, per), pl.ds(row, rows), :]

    barrier = pltpu.get_barrier_semaphore()
    for step in range(1, parts):
        @pl.when(polar)
        def _():
            pl.semaphore_signal(
                barrier, inc=1, device_id=(lax.rem(part + step, parts), band), device_id_type=MESH
            )
    for step in range(parts):
        pl.semaphore_signal(
            barrier,
            inc=1,
            device_id=(lax.rem(part + step, parts), jnp.where(polar, helper, source)),
            device_id_type=MESH,
        )

    loads = [
        pltpu.make_async_copy(tables.at[i], ref, local_sem.at[i])
        for i, ref in enumerate((high, low))
    ]
    for load in loads:
        load.start()
    through = pltpu.make_async_copy(state, out, local_sem.at[2])

    @pl.when(jnp.logical_not(polar))
    def _():
        through.start()
        pl.semaphore_wait(barrier, parts)

    @pl.when(polar)
    def _():
        pl.semaphore_wait(barrier, 2 * parts - 1)

        @pl.loop(0, chunks)
        def _(chunk):
            for step in range(parts):
                there = lax.rem(part + step, parts)
                pltpu.make_async_remote_copy(
                    src_ref=block(state, there + parts, chunk),
                    dst_ref=circles.at[chunk, part],
                    send_sem=send_sem.at[chunk, there + parts],
                    recv_sem=recv_sem.at[chunk, part],
                    device_id=(there, helper),
                    device_id_type=MESH,
                ).start()
                if step == 0:
                    pltpu.make_async_copy(
                        block(state, me, chunk), circles.at[chunk, part], recv_sem.at[chunk, part]
                    ).start()
                else:
                    pltpu.make_async_remote_copy(
                        src_ref=block(state, there, chunk),
                        dst_ref=circles.at[chunk, part],
                        send_sem=send_sem.at[chunk, there],
                        recv_sem=recv_sem.at[chunk, part],
                        device_id=(there, band),
                        device_id_type=MESH,
                    ).start()

    operand[...] = jnp.zeros_like(operand)
    for load in loads:
        load.wait()
    cos1, sin1, cos2, sin2 = (twists[i : i + 1, :] for i in range(4))
    half, whole = rows, per * rows

    @pl.loop(0, chunks)
    def _(chunk):
        for i in range(parts):
            slot = circles.at[chunk, i]
            pltpu.make_async_copy(slot, slot, recv_sem.at[chunk, i]).wait()
        q0, q1, q2, q3 = (circles[chunk, i].reshape(whole, quarter) for i in range(4))
        sum_a, sum_b, odd_a, odd_b = q0 + q2, q1 + q3, q0 - q2, q1 - q3
        skew = sum_a - sum_b
        skew_a, skew_b = skew[:half], skew[half:]
        stack = jnp.concatenate(
            [
                sum_a + sum_b,
                skew_a * cos2 + skew_b * sin2,
                skew_b * cos2 - skew_a * sin2,
                odd_a * cos1 - odd_b * sin1,
                -odd_a * sin1 - odd_b * cos1,
            ],
            axis=0,
        )
        split_store(operand, stack)
        product(operand, high, low, waves, False)
        row = pl.multiple_of((chunk % row_chunks) * rows, rows)
        g = [gains[i, pl.ds(row, rows), :] for i in range(5)]
        same0, same2, cross2, same1, cross1 = (
            g[0], g[1], g[2], jnp.concatenate([g[3]] * per), jnp.concatenate([g[4]] * per)
        )
        same0 = jnp.concatenate([same0] * per)
        cos_part, sin_part = waves[:, :lanes], waves[:, lanes:]
        two_a, two_b = slice(whole, whole + half), slice(whole + half, 2 * whole)
        one_a, one_b = slice(2 * whole, 3 * whole), slice(3 * whole, 4 * whole)
        rc2, rs2, ic2, is2 = mix(
            cos_part[two_a], sin_part[two_a], cos_part[two_b], sin_part[two_b], same2, cross2
        )
        rc1, rs1, ic1, is1 = mix(
            cos_part[one_a], sin_part[one_a], cos_part[one_b], sin_part[one_b], same1, cross1
        )
        damped = jnp.concatenate(
            [
                jnp.concatenate([same0 * cos_part[:whole], rc2, ic2, rc1, ic1], axis=0),
                jnp.concatenate([same0 * sin_part[:whole], rs2, is2, rs1, is1], axis=0),
            ],
            axis=1,
        )
        split_store(operand, damped)
        product(operand, high, low, waves, True)
        back = waves[:, :quarter]
        even, two_real, two_imag = back[:whole], back[two_a], back[two_b]
        one_real, one_imag = back[one_a], back[one_b]
        odd_a = one_real * cos1 - one_imag * sin1
        odd_b = -one_real * sin1 - one_imag * cos1
        skew = jnp.concatenate(
            [two_real * cos2 - two_imag * sin2, two_imag * cos2 + two_real * sin2], axis=0
        )
        plus, minus = even + skew, even - skew
        shape = (per, rows, quarter)
        results[chunk, 0] = (plus + odd_a).reshape(shape)
        results[chunk, 1] = (minus + odd_b).reshape(shape)
        results[chunk, 2] = (plus - odd_a).reshape(shape)
        results[chunk, 3] = (minus - odd_b).reshape(shape)
        if quarter < width:
            operand[:, quarter:] = jnp.zeros_like(operand[:, quarter:])
        for step in range(1, parts):
            there = lax.rem(part + step, parts)
            pltpu.make_async_remote_copy(
                src_ref=results.at[chunk, there],
                dst_ref=block(out, me, chunk),
                send_sem=back_send_sem.at[chunk, there],
                recv_sem=back_recv_sem.at[chunk, me],
                device_id=(there, source),
                device_id_type=MESH,
            ).start()

        @pl.when(polar)
        def _():
            pltpu.make_async_copy(
                results.at[chunk, part], block(out, me, chunk), back_recv_sem.at[chunk, me]
            ).start()

        @pl.when(jnp.logical_not(polar))
        def _():
            pltpu.make_async_remote_copy(
                src_ref=results.at[chunk, part],
                dst_ref=block(out, me, chunk),
                send_sem=back_send_sem.at[chunk, part],
                recv_sem=back_recv_sem.at[chunk, me],
                device_id=(part, source),
                device_id_type=MESH,
            ).start()

    def drain(ref, semaphore):
        pltpu.make_async_copy(ref, ref, semaphore).wait()

    @pl.loop(0, chunks)
    def _(chunk):
        for step in range(1, parts):
            there = lax.rem(part + step, parts)
            drain(results.at[chunk, there], back_send_sem.at[chunk, there])

        @pl.when(jnp.logical_not(polar))
        def _():
            drain(results.at[chunk, part], back_send_sem.at[chunk, part])

        @pl.when(polar)
        def _():
            for step in range(parts):
                there = lax.rem(part + step, parts)
                drain(block(state, there + parts, chunk), send_sem.at[chunk, there + parts])
                drain(block(out, there + parts, chunk), back_recv_sem.at[chunk, there + parts])
                drain(block(out, there, chunk), back_recv_sem.at[chunk, there])
                if step > 0:
                    drain(block(state, there, chunk), send_sem.at[chunk, there])

    @pl.when(jnp.logical_not(polar))
    def _():
        through.wait()


def shared_filter(work_block, cutoff):
    parts, bands = lax.axis_size("lon"), lax.axis_size("lat")
    components, levels, rows_here, quarter = work_block.shape
    state = work_block.reshape(components * levels, rows_here, quarter)
    per, rows = 2, 16
    chunks = (components * levels // (2 * parts) // per) * (rows_here // rows)
    basis = quarter_basis(quarter)
    width = basis.shape[1]
    square = np.zeros((width, width), np.float32)
    square[:quarter] = basis
    high = square.astype(jnp.bfloat16)
    low = (square - high.astype(np.float32)).astype(jnp.bfloat16)
    tables = jnp.asarray(np.stack([high, low]))
    cos_twist, sin_twist = quarter_twists(quarter)
    twists = jnp.asarray(np.stack([cos_twist[0], sin_twist[0], cos_twist[1], sin_twist[1]]))
    _, source, _ = worker_group(lax.axis_index("lat"), bands)
    row_cutoff = lax.dynamic_slice_in_dim(cutoff, source * rows_here, rows_here)
    same0, two, one = damping_tables(row_cutoff, quarter)
    gains = jnp.stack([same0, *two, *one])
    vmem, anywhere = pl.BlockSpec(memory_space=pltpu.VMEM), pl.BlockSpec(memory_space=pl.ANY)
    table = pltpu.VMEM((width, width), jnp.bfloat16)
    piece = pltpu.VMEM((chunks, parts, per, rows, quarter), jnp.float32)
    lines = 4 * per * rows
    out = pl.pallas_call(
        functools.partial(circle_kernel, bands, parts, chunks),
        out_shape=jax.ShapeDtypeStruct(state.shape, jnp.float32),
        in_specs=[anywhere, vmem, vmem, anywhere],
        out_specs=anywhere,
        scratch_shapes=[
            piece,
            piece,
            table,
            table,
            pltpu.VMEM((2 * lines, width), jnp.bfloat16),
            pltpu.VMEM((lines, width), jnp.float32),
            pltpu.SemaphoreType.DMA((chunks, 2 * parts)),
            pltpu.SemaphoreType.DMA((chunks, parts)),
            pltpu.SemaphoreType.DMA((chunks, parts)),
            pltpu.SemaphoreType.DMA((chunks, 2 * parts)),
            pltpu.SemaphoreType.DMA((3,)),
        ],
        compiler_params=pltpu.CompilerParams(
            collective_id=0, has_side_effects=True, vmem_limit_bytes=50 * 2**20
        ),
    )(state, gains, twists, tables)
    return out.reshape(work_block.shape)


def per_device(model_state, courant, cutoff):
    rows_here = model_state.shape[2]
    band_index = lax.axis_index("lat")
    extended = with_halo(model_state, (("lon", 3), ("lat", 2)), 1)
    extended = trim_rims(extended, 2)
    wind_east = extended[0]
    wind_north = extended[1]
    theta_ext = extended[2]
    thickness = extended[3]
    row_courant = courant[None, :, None]
    east_flux = wind_east * thickness
    north_flux = wind_north * thickness
    heat_content = theta_ext * thickness
    new_thickness = (
        thickness[:, 1:-1, 1:-1]
        - row_courant * along_lon(east_flux)
        - meridional_courant * along_lat(north_flux)
    )
    new_heat = (
        heat_content[:, 1:-1, 1:-1]
        - row_courant * along_lon(east_flux * theta_ext)
        - meridional_courant * along_lat(north_flux * theta_ext)
    )
    new_theta = new_heat / new_thickness
    heat_ext = trim_rims(with_halo(new_heat, (("lon", 2), ("lat", 1)), 1), 1)
    new_east = wind_east[:, 1:-1, 1:-1] - pressure_gain * row_courant * along_lon(heat_ext)
    new_north = wind_north[:, 1:-1, 1:-1] - pressure_gain * meridional_courant * along_lat(heat_ext)
    stacked = jnp.stack([new_east, new_north, new_theta, new_thickness])
    parts, bands = lax.axis_size("lon"), lax.axis_size("lat")
    planes = stacked.shape[0] * stacked.shape[1]
    if parts == 4 and bands % 4 == 0 and planes % (4 * parts) == 0 and rows_here % 16 == 0:
        return shared_filter(stacked, cutoff)
    own_cut = lax.dynamic_slice_in_dim(cutoff, band_index * rows_here, rows_here)
    return filter_block(stacked, own_cut)


def solution(mesh):
    placed = (P(None, None, "lat", "lon"), P("lat"), P())
    return jax.shard_map(
        per_device,
        mesh=mesh,
        in_specs=placed,
        out_specs=P(None, None, "lat", "lon"),
        check_vma=False,
    )
```

```python
import functools

import jax
import jax.numpy as jnp
import numpy as np
from jax import lax
from jax.experimental import pallas as pl
from jax.experimental.pallas import tpu as pltpu
from jax.sharding import PartitionSpec as P

meridional_courant = 0.05
pressure_gain = 4.0
MESH = pl.DeviceIdType.MESH


def with_halo(array, sides, width):
    for axis, dim in sides:
        size, length = (lax.axis_size(axis), array.shape[dim])
        up = [(i, (i + 1) % size) for i in range(size)]
        down = [(j, i) for i, j in up]
        last = lax.slice_in_dim(array, length - width, length, axis=dim)
        first = lax.slice_in_dim(array, 0, width, axis=dim)
        before = lax.ppermute(last, axis, up)
        after = lax.ppermute(first, axis, down)
        array = jnp.concatenate([before, array, after], axis=dim)
    return array


def quarter_basis(quarter):
    half = quarter // 2
    lanes = -(-(half + 1) // 128) * 128
    phase = np.outer(np.arange(quarter), np.arange(half + 1)) % quarter
    angle = 2.0 * np.pi / quarter * phase
    table = np.zeros((quarter, 2 * lanes), np.float32)
    table[:, : half + 1] = np.cos(angle)
    table[:, lanes : lanes + half + 1] = np.sin(angle)
    return table


def quarter_twists(quarter):
    angle = 2.0 * np.pi / (4 * quarter) * np.outer([1.0, 2.0], np.arange(quarter))
    return np.cos(angle).astype(np.float32), np.sin(angle).astype(np.float32)


def damping_tables(row_cutoff, quarter):
    half = quarter // 2
    length = 4 * quarter
    lanes = -(-(half + 1) // 128) * 128
    index = jnp.arange(lanes, dtype=jnp.int32)
    inside = index <= half
    weight = jnp.where(inside, jnp.where((index == 0) | (index == half), 1.0, 2.0), 0.0) / quarter
    cut = row_cutoff.astype(jnp.float32)[:, None]

    def damping(wave_number):
        wave_number = jnp.abs(wave_number)
        folded = jnp.minimum(wave_number, length - wave_number)
        ratio = cut / jnp.maximum(folded, 1).astype(jnp.float32)[None, :]
        return jnp.minimum(1.0, ratio * ratio)

    def pair(shift, scale):
        above = damping(4 * index + shift)
        below = damping(4 * index - shift)
        gain = weight[None, :] * (0.5 * scale)
        return gain * (above + below), gain * (above - below)

    return pair(0, 0.25)[0], pair(2, 0.25), pair(1, 0.5)


def mix(real_cos, real_sin, imag_cos, imag_sin, same, cross):
    return (
        same * real_cos + cross * imag_sin,
        same * real_sin - cross * imag_cos,
        same * imag_cos - cross * real_sin,
        same * imag_sin + cross * real_cos,
    )


def damp_quarters(quarters, row_cutoff):
    _, planes, rows, quarter = quarters.shape
    basis = jnp.asarray(quarter_basis(quarter))
    cos_twist, sin_twist = quarter_twists(quarter)
    q0, q1, q2, q3 = quarters
    even, odd_a, odd_b = (q0 + q2) + (q1 + q3), q0 - q2, q1 - q3
    skew = (q0 + q2) - (q1 + q3)
    pairs = planes // 2
    skew_a, skew_b = skew[:pairs], skew[pairs:]
    one_real = odd_a * cos_twist[0] - odd_b * sin_twist[0]
    one_imag = -odd_a * sin_twist[0] - odd_b * cos_twist[0]
    two_real = skew_a * cos_twist[1] + skew_b * sin_twist[1]
    two_imag = skew_b * cos_twist[1] - skew_a * sin_twist[1]
    stack = jnp.concatenate([even, two_real, two_imag, one_real, one_imag], axis=0)
    waves = jnp.einsum("prm,mk->prk", stack, basis, precision=lax.Precision.HIGH)
    lanes = basis.shape[1] // 2
    cos_part, sin_part = waves[..., :lanes], waves[..., lanes:]
    same0, (same2, cross2), (same1, cross1) = damping_tables(row_cutoff, quarter)
    p, h = planes, pairs
    two = slice(p, p + h), slice(p + h, 2 * p)
    one = slice(2 * p, 3 * p), slice(3 * p, 4 * p)
    even_c, even_s = same0 * cos_part[:p], same0 * sin_part[:p]
    rc2, rs2, ic2, is2 = mix(
        cos_part[two[0]], sin_part[two[0]], cos_part[two[1]], sin_part[two[1]], same2, cross2
    )
    rc1, rs1, ic1, is1 = mix(
        cos_part[one[0]], sin_part[one[0]], cos_part[one[1]], sin_part[one[1]], same1, cross1
    )
    damped = jnp.concatenate(
        [
            jnp.concatenate([even_c, rc2, ic2, rc1, ic1], axis=0),
            jnp.concatenate([even_s, rs2, is2, rs1, is1], axis=0),
        ],
        axis=-1,
    )
    back = jnp.einsum("prk,mk->prm", damped, basis, precision=lax.Precision.HIGH)
    even, two_real, two_imag = back[:p], back[two[0]], back[two[1]]
    one_real, one_imag = back[one[0]], back[one[1]]
    odd_a = one_real * cos_twist[0] - one_imag * sin_twist[0]
    odd_b = -one_real * sin_twist[0] - one_imag * cos_twist[0]
    skew = jnp.concatenate(
        [
            two_real * cos_twist[1] - two_imag * sin_twist[1],
            two_imag * cos_twist[1] + two_real * sin_twist[1],
        ],
        axis=0,
    )
    plus, minus = even + skew, even - skew
    return jnp.stack([plus + odd_a, minus + odd_b, plus - odd_a, minus - odd_b])


def trim_rims(extended, row_dim):
    band_index = lax.axis_index("lat")
    band_count = lax.axis_size("lat")
    rows_ext = extended.shape[row_dim]
    positions = jnp.arange(rows_ext, dtype=jnp.int32)
    keep_rows = jnp.logical_not(
        (positions == 0) & (band_index == 0)
        | (positions == rows_ext - 1) & (band_index == band_count - 1)
    )
    mask_shape = [1] * extended.ndim
    mask_shape[row_dim] = rows_ext
    return extended * keep_rows.astype(extended.dtype).reshape(mask_shape)


def along_lon(field_ext):
    return (field_ext[..., 1:-1, 2:] - field_ext[..., 1:-1, :-2]) * 0.5


def along_lat(field_ext):
    return (field_ext[..., 2:, 1:-1] - field_ext[..., :-2, 1:-1]) * 0.5


def filter_block(work_block, block_cutoff):
    lon_parts = lax.axis_size("lon")
    components, levels, rows_here, width_here = work_block.shape
    planes = components * levels // lon_parts
    group = lon_parts // 4
    lines = work_block.reshape(lon_parts, planes, rows_here, width_here)
    circles = lax.all_to_all(lines, "lon", split_axis=0, concat_axis=0, tiled=True)
    quarters = circles.reshape(4, group, planes, rows_here, width_here)
    quarters = jnp.moveaxis(quarters, 1, 3).reshape(4, planes, rows_here, group * width_here)
    smoothed = damp_quarters(quarters, block_cutoff)
    smoothed = smoothed.reshape(4, planes, rows_here, group, width_here)
    smoothed = jnp.moveaxis(smoothed, 3, 1).reshape(lines.shape)
    returned = lax.all_to_all(smoothed, "lon", split_axis=0, concat_axis=0, tiled=True)
    return returned.reshape(work_block.shape)


def worker_group(band, bands):
    quarter = bands // 4
    low = band < bands // 2
    polar = jnp.logical_or(band < quarter, band >= bands - quarter)
    inner = jnp.where(low, band - quarter, band + quarter)
    source = jnp.where(polar, band, inner)
    helper = jnp.where(source < bands // 2, source + quarter, source - quarter)
    return polar, source, helper


def split_store(ref, values):
    rows, width = values.shape
    high = values.astype(jnp.bfloat16)
    low = (values - high.astype(jnp.float32)).astype(jnp.bfloat16)
    ref[:rows, :width] = high
    ref[rows:, :width] = low


def product(parts, high_ref, low_ref, out_ref, back):
    rows = out_ref.shape[0]
    dims = (((1,), (1 if back else 0,)), ((), ()))
    for start in range(0, out_ref.shape[1], 256):
        cols = slice(start, start + 256)
        piece = (cols, slice(None)) if back else (slice(None), cols)
        both = lax.dot_general(parts[...], high_ref[piece], dims, preferred_element_type=jnp.float32)
        cross = lax.dot_general(
            parts[:rows, :], low_ref[piece], dims, preferred_element_type=jnp.float32
        )
        out_ref[:, cols] = (both[:rows] + both[rows:]) + cross


def circle_kernel(
    bands, parts, chunks, state, gains, twists, tables, out, circles, results, high, low, operand, waves,
    send_sem, recv_sem, back_send_sem, back_recv_sem, local_sem,
):
    part = lax.axis_index("lon")
    band = lax.axis_index("lat")
    polar, source, helper = worker_group(band, bands)
    _, _, per, rows, quarter = circles.shape
    width = high.shape[1]
    lanes = width // 2
    workers = 2 * parts
    row_chunks = state.shape[1] // rows
    planes_per = state.shape[0] // workers
    me = jnp.where(polar, part, part + parts)

    def block(ref, worker, chunk):
        plane = worker * planes_per + (chunk // row_chunks) * per
        row = pl.multiple_of((chunk % row_chunks) * rows, rows)
        return ref.at[pl.ds(plane, per), pl.ds(row, rows), :]

    barrier = pltpu.get_barrier_semaphore()
    for step in range(1, parts):
        @pl.when(polar)
        def _():
            pl.semaphore_signal(
                barrier, inc=1, device_id=(lax.rem(part + step, parts), band), device_id_type=MESH
            )
    for step in range(parts):
        pl.semaphore_signal(
            barrier,
            inc=1,
            device_id=(lax.rem(part + step, parts), jnp.where(polar, helper, source)),
            device_id_type=MESH,
        )

    loads = [
        pltpu.make_async_copy(tables.at[i], ref, local_sem.at[i])
        for i, ref in enumerate((high, low))
    ]
    for load in loads:
        load.start()
    through = pltpu.make_async_copy(state, out, local_sem.at[2])

    @pl.when(jnp.logical_not(polar))
    def _():
        through.start()
        pl.semaphore_wait(barrier, parts)

    @pl.when(polar)
    def _():
        pl.semaphore_wait(barrier, 2 * parts - 1)

        @pl.loop(0, chunks)
        def _(chunk):
            for step in range(parts):
                there = lax.rem(part + step, parts)
                pltpu.make_async_remote_copy(
                    src_ref=block(state, there + parts, chunk),
                    dst_ref=circles.at[chunk, part],
                    send_sem=send_sem.at[chunk, there + parts],
                    recv_sem=recv_sem.at[chunk, part],
                    device_id=(there, helper),
                    device_id_type=MESH,
                ).start()
                if step == 0:
                    pltpu.make_async_copy(
                        block(state, me, chunk), circles.at[chunk, part], recv_sem.at[chunk, part]
                    ).start()
                else:
                    pltpu.make_async_remote_copy(
                        src_ref=block(state, there, chunk),
                        dst_ref=circles.at[chunk, part],
                        send_sem=send_sem.at[chunk, there],
                        recv_sem=recv_sem.at[chunk, part],
                        device_id=(there, band),
                        device_id_type=MESH,
                    ).start()

    operand[...] = jnp.zeros_like(operand)
    for load in loads:
        load.wait()
    cos1, sin1, cos2, sin2 = (twists[i : i + 1, :] for i in range(4))
    half, whole = rows, per * rows

    @pl.loop(0, chunks)
    def _(chunk):
        for i in range(parts):
            slot = circles.at[chunk, i]
            pltpu.make_async_copy(slot, slot, recv_sem.at[chunk, i]).wait()
        q0, q1, q2, q3 = (circles[chunk, i].reshape(whole, quarter) for i in range(4))
        sum_a, sum_b, odd_a, odd_b = q0 + q2, q1 + q3, q0 - q2, q1 - q3
        skew = sum_a - sum_b
        skew_a, skew_b = skew[:half], skew[half:]
        stack = jnp.concatenate(
            [
                sum_a + sum_b,
                skew_a * cos2 + skew_b * sin2,
                skew_b * cos2 - skew_a * sin2,
                odd_a * cos1 - odd_b * sin1,
                -odd_a * sin1 - odd_b * cos1,
            ],
            axis=0,
        )
        split_store(operand, stack)
        product(operand, high, low, waves, False)
        row = pl.multiple_of((chunk % row_chunks) * rows, rows)
        g = [gains[i, pl.ds(row, rows), :] for i in range(5)]
        same0, same2, cross2, same1, cross1 = (
            g[0], g[1], g[2], jnp.concatenate([g[3]] * per), jnp.concatenate([g[4]] * per)
        )
        same0 = jnp.concatenate([same0] * per)
        cos_part, sin_part = waves[:, :lanes], waves[:, lanes:]
        two_a, two_b = slice(whole, whole + half), slice(whole + half, 2 * whole)
        one_a, one_b = slice(2 * whole, 3 * whole), slice(3 * whole, 4 * whole)
        rc2, rs2, ic2, is2 = mix(
            cos_part[two_a], sin_part[two_a], cos_part[two_b], sin_part[two_b], same2, cross2
        )
        rc1, rs1, ic1, is1 = mix(
            cos_part[one_a], sin_part[one_a], cos_part[one_b], sin_part[one_b], same1, cross1
        )
        damped = jnp.concatenate(
            [
                jnp.concatenate([same0 * cos_part[:whole], rc2, ic2, rc1, ic1], axis=0),
                jnp.concatenate([same0 * sin_part[:whole], rs2, is2, rs1, is1], axis=0),
            ],
            axis=1,
        )
        split_store(operand, damped)
        product(operand, high, low, waves, True)
        back = waves[:, :quarter]
        even, two_real, two_imag = back[:whole], back[two_a], back[two_b]
        one_real, one_imag = back[one_a], back[one_b]
        odd_a = one_real * cos1 - one_imag * sin1
        odd_b = -one_real * sin1 - one_imag * cos1
        skew = jnp.concatenate(
            [two_real * cos2 - two_imag * sin2, two_imag * cos2 + two_real * sin2], axis=0
        )
        plus, minus = even + skew, even - skew
        shape = (per, rows, quarter)
        results[chunk, 0] = (plus + odd_a).reshape(shape)
        results[chunk, 1] = (minus + odd_b).reshape(shape)
        results[chunk, 2] = (plus - odd_a).reshape(shape)
        results[chunk, 3] = (minus - odd_b).reshape(shape)
        if quarter < width:
            operand[:, quarter:] = jnp.zeros_like(operand[:, quarter:])
        for step in range(1, parts):
            there = lax.rem(part + step, parts)
            pltpu.make_async_remote_copy(
                src_ref=results.at[chunk, there],
                dst_ref=block(out, me, chunk),
                send_sem=back_send_sem.at[chunk, there],
                recv_sem=back_recv_sem.at[chunk, me],
                device_id=(there, source),
                device_id_type=MESH,
            ).start()

        @pl.when(polar)
        def _():
            pltpu.make_async_copy(
                results.at[chunk, part], block(out, me, chunk), back_recv_sem.at[chunk, me]
            ).start()

        @pl.when(jnp.logical_not(polar))
        def _():
            pltpu.make_async_remote_copy(
                src_ref=results.at[chunk, part],
                dst_ref=block(out, me, chunk),
                send_sem=back_send_sem.at[chunk, part],
                recv_sem=back_recv_sem.at[chunk, me],
                device_id=(part, source),
                device_id_type=MESH,
            ).start()

    def drain(ref, semaphore):
        pltpu.make_async_copy(ref, ref, semaphore).wait()

    @pl.loop(0, chunks)
    def _(chunk):
        for step in range(1, parts):
            there = lax.rem(part + step, parts)
            drain(results.at[chunk, there], back_send_sem.at[chunk, there])

        @pl.when(jnp.logical_not(polar))
        def _():
            drain(results.at[chunk, part], back_send_sem.at[chunk, part])

        @pl.when(polar)
        def _():
            for step in range(parts):
                there = lax.rem(part + step, parts)
                drain(block(state, there + parts, chunk), send_sem.at[chunk, there + parts])
                drain(block(out, there + parts, chunk), back_recv_sem.at[chunk, there + parts])
                drain(block(out, there, chunk), back_recv_sem.at[chunk, there])
                if step > 0:
                    drain(block(state, there, chunk), send_sem.at[chunk, there])

    @pl.when(jnp.logical_not(polar))
    def _():
        through.wait()


def shared_filter(work_block, cutoff):
    parts, bands = lax.axis_size("lon"), lax.axis_size("lat")
    components, levels, rows_here, quarter = work_block.shape
    state = work_block.reshape(components * levels, rows_here, quarter)
    per, rows = 2, 16
    chunks = (components * levels // (2 * parts) // per) * (rows_here // rows)
    basis = quarter_basis(quarter)
    width = basis.shape[1]
    square = np.zeros((width, width), np.float32)
    square[:quarter] = basis
    high = square.astype(jnp.bfloat16)
    low = (square - high.astype(np.float32)).astype(jnp.bfloat16)
    tables = jnp.asarray(np.stack([high, low]))
    cos_twist, sin_twist = quarter_twists(quarter)
    twists = jnp.asarray(np.stack([cos_twist[0], sin_twist[0], cos_twist[1], sin_twist[1]]))
    _, source, _ = worker_group(lax.axis_index("lat"), bands)
    row_cutoff = lax.dynamic_slice_in_dim(cutoff, source * rows_here, rows_here)
    same0, two, one = damping_tables(row_cutoff, quarter)
    gains = jnp.stack([same0, *two, *one])
    vmem, anywhere = pl.BlockSpec(memory_space=pltpu.VMEM), pl.BlockSpec(memory_space=pl.ANY)
    table = pltpu.VMEM((width, width), jnp.bfloat16)
    piece = pltpu.VMEM((chunks, parts, per, rows, quarter), jnp.float32)
    lines = 4 * per * rows
    out = pl.pallas_call(
        functools.partial(circle_kernel, bands, parts, chunks),
        out_shape=jax.ShapeDtypeStruct(state.shape, jnp.float32),
        in_specs=[vmem, vmem, vmem, anywhere],
        out_specs=anywhere,
        scratch_shapes=[
            piece,
            piece,
            table,
            table,
            pltpu.VMEM((2 * lines, width), jnp.bfloat16),
            pltpu.VMEM((lines, width), jnp.float32),
            pltpu.SemaphoreType.DMA((chunks, 2 * parts)),
            pltpu.SemaphoreType.DMA((chunks, parts)),
            pltpu.SemaphoreType.DMA((chunks, parts)),
            pltpu.SemaphoreType.DMA((chunks, 2 * parts)),
            pltpu.SemaphoreType.DMA((3,)),
        ],
        compiler_params=pltpu.CompilerParams(
            collective_id=0, has_side_effects=True, vmem_limit_bytes=50 * 2**20
        ),
    )(state, gains, twists, tables)
    return out.reshape(work_block.shape)


def per_device(model_state, courant, cutoff):
    rows_here = model_state.shape[2]
    band_index = lax.axis_index("lat")
    extended = with_halo(model_state, (("lon", 3), ("lat", 2)), 1)
    extended = trim_rims(extended, 2)
    wind_east = extended[0]
    wind_north = extended[1]
    theta_ext = extended[2]
    thickness = extended[3]
    row_courant = courant[None, :, None]
    east_flux = wind_east * thickness
    north_flux = wind_north * thickness
    heat_content = theta_ext * thickness
    new_thickness = (
        thickness[:, 1:-1, 1:-1]
        - row_courant * along_lon(east_flux)
        - meridional_courant * along_lat(north_flux)
    )
    new_heat = (
        heat_content[:, 1:-1, 1:-1]
        - row_courant * along_lon(east_flux * theta_ext)
        - meridional_courant * along_lat(north_flux * theta_ext)
    )
    new_theta = new_heat / new_thickness
    heat_ext = trim_rims(with_halo(new_heat, (("lon", 2), ("lat", 1)), 1), 1)
    new_east = wind_east[:, 1:-1, 1:-1] - pressure_gain * row_courant * along_lon(heat_ext)
    new_north = wind_north[:, 1:-1, 1:-1] - pressure_gain * meridional_courant * along_lat(heat_ext)
    stacked = jnp.stack([new_east, new_north, new_theta, new_thickness])
    parts, bands = lax.axis_size("lon"), lax.axis_size("lat")
    planes = stacked.shape[0] * stacked.shape[1]
    if parts == 4 and bands % 4 == 0 and planes % (4 * parts) == 0 and rows_here % 16 == 0:
        return shared_filter(stacked, cutoff)
    own_cut = lax.dynamic_slice_in_dim(cutoff, band_index * rows_here, rows_here)
    return filter_block(stacked, own_cut)


def solution(mesh):
    placed = (P(None, None, "lat", "lon"), P("lat"), P())
    return jax.shard_map(
        per_device,
        mesh=mesh,
        in_specs=placed,
        out_specs=P(None, None, "lat", "lon"),
        check_vma=False,
    )
```

```python
import functools

import jax
import jax.numpy as jnp
import numpy as np
from jax import lax
from jax.experimental import pallas as pl
from jax.experimental.pallas import tpu as pltpu
from jax.sharding import PartitionSpec as P

meridional_courant = 0.05
pressure_gain = 4.0
courant_lane = 64
MESH = pl.DeviceIdType.MESH


def with_halo(array, sides, width):
    for axis, dim in sides:
        size, length = (lax.axis_size(axis), array.shape[dim])
        up = [(i, (i + 1) % size) for i in range(size)]
        down = [(j, i) for i, j in up]
        last = lax.slice_in_dim(array, length - width, length, axis=dim)
        first = lax.slice_in_dim(array, 0, width, axis=dim)
        before = lax.ppermute(last, axis, up)
        after = lax.ppermute(first, axis, down)
        array = jnp.concatenate([before, array, after], axis=dim)
    return array


def quarter_basis(quarter):
    half = quarter // 2
    lanes = -(-(half + 1) // 128) * 128
    phase = np.outer(np.arange(quarter), np.arange(half + 1)) % quarter
    angle = 2.0 * np.pi / quarter * phase
    table = np.zeros((quarter, 2 * lanes), np.float32)
    table[:, : half + 1] = np.cos(angle)
    table[:, lanes : lanes + half + 1] = np.sin(angle)
    return table


def quarter_twists(quarter):
    angle = 2.0 * np.pi / (4 * quarter) * np.outer([1.0, 2.0], np.arange(quarter))
    return np.cos(angle).astype(np.float32), np.sin(angle).astype(np.float32)


def damping_tables(row_cutoff, quarter):
    half = quarter // 2
    length = 4 * quarter
    lanes = -(-(half + 1) // 128) * 128
    index = jnp.arange(lanes, dtype=jnp.int32)
    inside = index <= half
    weight = jnp.where(inside, jnp.where((index == 0) | (index == half), 1.0, 2.0), 0.0) / quarter
    cut = row_cutoff.astype(jnp.float32)[:, None]

    def damping(wave_number):
        wave_number = jnp.abs(wave_number)
        folded = jnp.minimum(wave_number, length - wave_number)
        ratio = cut / jnp.maximum(folded, 1).astype(jnp.float32)[None, :]
        return jnp.minimum(1.0, ratio * ratio)

    def pair(shift, scale):
        above = damping(4 * index + shift)
        below = damping(4 * index - shift)
        gain = weight[None, :] * (0.5 * scale)
        return gain * (above + below), gain * (above - below)

    return pair(0, 0.25)[0], pair(2, 0.25), pair(1, 0.5)


def mix(real_cos, real_sin, imag_cos, imag_sin, same, cross):
    return (
        same * real_cos + cross * imag_sin,
        same * real_sin - cross * imag_cos,
        same * imag_cos - cross * real_sin,
        same * imag_sin + cross * real_cos,
    )


def damp_quarters(quarters, row_cutoff):
    _, planes, rows, quarter = quarters.shape
    basis = jnp.asarray(quarter_basis(quarter))
    cos_twist, sin_twist = quarter_twists(quarter)
    q0, q1, q2, q3 = quarters
    even, odd_a, odd_b = (q0 + q2) + (q1 + q3), q0 - q2, q1 - q3
    skew = (q0 + q2) - (q1 + q3)
    pairs = planes // 2
    skew_a, skew_b = skew[:pairs], skew[pairs:]
    one_real = odd_a * cos_twist[0] - odd_b * sin_twist[0]
    one_imag = -odd_a * sin_twist[0] - odd_b * cos_twist[0]
    two_real = skew_a * cos_twist[1] + skew_b * sin_twist[1]
    two_imag = skew_b * cos_twist[1] - skew_a * sin_twist[1]
    stack = jnp.concatenate([even, two_real, two_imag, one_real, one_imag], axis=0)
    waves = jnp.einsum("prm,mk->prk", stack, basis, precision=lax.Precision.HIGH)
    lanes = basis.shape[1] // 2
    cos_part, sin_part = waves[..., :lanes], waves[..., lanes:]
    same0, (same2, cross2), (same1, cross1) = damping_tables(row_cutoff, quarter)
    p, h = planes, pairs
    two = slice(p, p + h), slice(p + h, 2 * p)
    one = slice(2 * p, 3 * p), slice(3 * p, 4 * p)
    even_c, even_s = same0 * cos_part[:p], same0 * sin_part[:p]
    rc2, rs2, ic2, is2 = mix(
        cos_part[two[0]], sin_part[two[0]], cos_part[two[1]], sin_part[two[1]], same2, cross2
    )
    rc1, rs1, ic1, is1 = mix(
        cos_part[one[0]], sin_part[one[0]], cos_part[one[1]], sin_part[one[1]], same1, cross1
    )
    damped = jnp.concatenate(
        [
            jnp.concatenate([even_c, rc2, ic2, rc1, ic1], axis=0),
            jnp.concatenate([even_s, rs2, is2, rs1, is1], axis=0),
        ],
        axis=-1,
    )
    back = jnp.einsum("prk,mk->prm", damped, basis, precision=lax.Precision.HIGH)
    even, two_real, two_imag = back[:p], back[two[0]], back[two[1]]
    one_real, one_imag = back[one[0]], back[one[1]]
    odd_a = one_real * cos_twist[0] - one_imag * sin_twist[0]
    odd_b = -one_real * sin_twist[0] - one_imag * cos_twist[0]
    skew = jnp.concatenate(
        [
            two_real * cos_twist[1] - two_imag * sin_twist[1],
            two_imag * cos_twist[1] + two_real * sin_twist[1],
        ],
        axis=0,
    )
    plus, minus = even + skew, even - skew
    return jnp.stack([plus + odd_a, minus + odd_b, plus - odd_a, minus - odd_b])


def trim_rims(extended, row_dim):
    band_index = lax.axis_index("lat")
    band_count = lax.axis_size("lat")
    rows_ext = extended.shape[row_dim]
    positions = jnp.arange(rows_ext, dtype=jnp.int32)
    keep_rows = jnp.logical_not(
        (positions == 0) & (band_index == 0)
        | (positions == rows_ext - 1) & (band_index == band_count - 1)
    )
    mask_shape = [1] * extended.ndim
    mask_shape[row_dim] = rows_ext
    return extended * keep_rows.astype(extended.dtype).reshape(mask_shape)


def along_lon(field_ext):
    return (field_ext[..., 1:-1, 2:] - field_ext[..., 1:-1, :-2]) * 0.5


def along_lat(field_ext):
    return (field_ext[..., 2:, 1:-1] - field_ext[..., :-2, 1:-1]) * 0.5


def filter_block(work_block, block_cutoff):
    lon_parts = lax.axis_size("lon")
    components, levels, rows_here, width_here = work_block.shape
    planes = components * levels // lon_parts
    group = lon_parts // 4
    lines = work_block.reshape(lon_parts, planes, rows_here, width_here)
    circles = lax.all_to_all(lines, "lon", split_axis=0, concat_axis=0, tiled=True)
    quarters = circles.reshape(4, group, planes, rows_here, width_here)
    quarters = jnp.moveaxis(quarters, 1, 3).reshape(4, planes, rows_here, group * width_here)
    smoothed = damp_quarters(quarters, block_cutoff)
    smoothed = smoothed.reshape(4, planes, rows_here, group, width_here)
    smoothed = jnp.moveaxis(smoothed, 3, 1).reshape(lines.shape)
    returned = lax.all_to_all(smoothed, "lon", split_axis=0, concat_axis=0, tiled=True)
    return returned.reshape(work_block.shape)


def worker_group(band, bands):
    quarter = bands // 4
    low = band < bands // 2
    polar = jnp.logical_or(band < quarter, band >= bands - quarter)
    inner = jnp.where(low, band - quarter, band + quarter)
    source = jnp.where(polar, band, inner)
    helper = jnp.where(source < bands // 2, source + quarter, source - quarter)
    return polar, source, helper


def split_store(ref, values):
    rows, width = values.shape
    high = values.astype(jnp.bfloat16)
    low = (values - high.astype(jnp.float32)).astype(jnp.bfloat16)
    ref[:rows, :width] = high
    ref[rows:, :width] = low


def product(parts, high_ref, low_ref, out_ref, back):
    rows = out_ref.shape[0]
    dims = (((1,), (1 if back else 0,)), ((), ()))
    for start in range(0, out_ref.shape[1], 256):
        cols = slice(start, start + 256)
        piece = (cols, slice(None)) if back else (slice(None), cols)
        both = lax.dot_general(parts[...], high_ref[piece], dims, preferred_element_type=jnp.float32)
        cross = lax.dot_general(
            parts[:rows, :], low_ref[piece], dims, preferred_element_type=jnp.float32
        )
        out_ref[:, cols] = (both[:rows] + both[rows:]) + cross


def edge_tile(state, ring, courant, component, level, rows):
    rest = state.shape[3] % 128
    tail = state[component, level, rows, state.shape[3] - rest :]
    count = tail.shape[0]
    tail = jnp.concatenate([tail, jnp.zeros((count, 128 - rest), jnp.float32)], axis=1)
    lane = lax.broadcasted_iota(jnp.int32, (count, 128), 1)
    tile = jnp.where(lane == courant_lane, courant[rows, :], tail)
    tile = jnp.where((lane == rest) | (lane == rest + 1), ring[1, component, level, rows, :], tile)
    return jnp.where(lane >= 126, ring[0, component, level, rows, :], tile)


def substep_level(state, ring, caps, courant, field, work, level, first, last):
    components, levels, rows, quarter = state.shape
    width = field.shape[2]
    body = width - 128
    for c in range(components):
        field[c, 8 : 8 + rows, :body] = state[c, level, :, :body]
        field[c, 8 : 8 + rows, body:] = edge_tile(state, ring, courant, c, level, slice(0, rows))
        field[c, 6:8, :] = caps[0, 2 * (c * levels + level) : 2 * (c * levels + level) + 2, :]
        field[c, 8 + rows : 10 + rows, :] = caps[1, 2 * (c * levels + level) : 2 * (c * levels + level) + 2, :]
    east, north, theta, thick = (field[c] for c in range(4))
    height = east.shape[0]
    row_courant = east[:, body + courant_lane : body + courant_lane + 1]

    def along_x(f):
        return (pltpu.roll(f, width - 1, 1) - pltpu.roll(f, 1, 1)) * 0.5

    def along_y(f):
        return (pltpu.roll(f, height - 1, 0) - pltpu.roll(f, 1, 0)) * 0.5

    east_flux, north_flux = east * thick, north * thick
    new_thick = thick - row_courant * along_x(east_flux) - meridional_courant * along_y(north_flux)
    heat = (
        theta * thick
        - row_courant * along_x(east_flux * theta)
        - meridional_courant * along_y(north_flux * theta)
    )
    row = lax.broadcasted_iota(jnp.int32, (height, 1), 0)
    beyond = (first & (row < 8)) | (last & (row >= 8 + rows))
    heat = jnp.where(beyond, 0.0, heat)
    new_east = east - pressure_gain * row_courant * along_x(heat)
    new_north = north - pressure_gain * meridional_courant * along_y(heat)
    own = slice(8, 8 + rows)
    work[0, level] = new_east[own, :quarter]
    work[1, level] = new_north[own, :quarter]
    work[2, level] = heat[own, :quarter] / new_thick[own, :quarter]
    work[3, level] = new_thick[own, :quarter]


def circle_kernel(
    bands, parts, chunks, state, courant, gains, twists, table, out, circles, results, basis, high, low,
    operand, waves, pack, ring, edges, caps, field, work,
    send_sem, recv_sem, back_send_sem, back_recv_sem, local_sem, halo_send, halo_recv,
):
    part = lax.axis_index("lon")
    band = lax.axis_index("lat")
    polar, source, helper = worker_group(band, bands)
    _, _, per, rows, quarter = circles.shape
    components, levels, rows_here, _ = state.shape
    width = high.shape[1]
    lanes = width // 2
    row_chunks = rows_here // rows
    me = jnp.where(polar, part, part + parts)
    first, last = band == 0, band == bands - 1

    def block(ref, worker, chunk):
        level = (chunk // row_chunks) * 2 * per + (worker // parts) * per
        row = pl.multiple_of((chunk % row_chunks) * rows, rows)
        return ref.at[lax.rem(worker, parts), pl.ds(level, per), pl.ds(row, rows), :]

    load = pltpu.make_async_copy(table, basis, local_sem.at[0])
    load.start()

    caps[...] = jnp.zeros_like(caps)
    barrier = pltpu.get_barrier_semaphore()

    def greet(there, row_band):
        pl.semaphore_signal(barrier, inc=1, device_id=(there, row_band), device_id_type=MESH)

    for step in range(1, parts):
        greet(lax.rem(part + step, parts), band)
    for step in range(parts):
        greet(lax.rem(part + step, parts), jnp.where(polar, helper, source))

    @pl.when(band > 0)
    def _():
        greet(part, band - 1)

    @pl.when(band < bands - 1)
    def _():
        greet(part, band + 1)

    rest = quarter % 128
    lane = lax.broadcasted_iota(jnp.int32, (rows_here, 128), 1)

    @pl.loop(0, levels)
    def _(level):
        for c in range(components):
            begin = pltpu.roll(state[c, level, :, :128], rest, 1)
            tail = state[c, level, :, quarter - rest :]
            tail = jnp.concatenate([tail, jnp.zeros((rows_here, 128 - rest), jnp.float32)], axis=1)
            pack[c, level] = jnp.where(lane >= 126, pltpu.roll(tail, 128 - rest, 1), begin)

    inner_bands = jnp.where(first | last, 1, 2)
    pl.semaphore_wait(barrier, 2 * parts - 1 + inner_bands)
    columns = [
        pltpu.make_async_remote_copy(
            src_ref=pack,
            dst_ref=ring.at[slot],
            send_sem=halo_send.at[slot],
            recv_sem=halo_recv.at[slot],
            device_id=(lax.rem(part + shift, parts), band),
            device_id_type=MESH,
        )
        for slot, shift in ((0, 1), (1, parts - 1))
    ]
    for copy in columns:
        copy.start()
    field[...] = jnp.zeros_like(field)
    operand[...] = jnp.zeros_like(operand)
    load.wait()

    @pl.loop(0, width // 32)
    def _(step):
        at = pl.ds(pl.multiple_of(step * 32, 32), 32)
        exact = basis[at, :]
        upper = exact.astype(jnp.bfloat16)
        high[at, :] = upper
        low[at, :] = (exact - upper.astype(jnp.float32)).astype(jnp.bfloat16)

    for copy in columns:
        copy.wait()

    body = width - 128
    for c in range(components):
        for level in range(levels):
            at = slice(2 * (c * levels + level), 2 * (c * levels + level) + 2)
            for slot, own in ((0, slice(rows_here - 2, rows_here)), (1, slice(0, 2))):
                edges[slot, at, :body] = state[c, level, own, :body]
                edges[slot, at, body:] = edge_tile(state, ring, courant, c, level, own)

    def rows_to(slot, row_band):
        return pltpu.make_async_remote_copy(
            src_ref=edges.at[slot],
            dst_ref=caps.at[slot],
            send_sem=halo_send.at[2 + slot],
            recv_sem=halo_recv.at[2 + slot],
            device_id=(part, row_band),
            device_id_type=MESH,
        )

    @pl.when(jnp.logical_not(last))
    def _():
        rows_to(0, band + 1).start()

    @pl.when(jnp.logical_not(first))
    def _():
        rows_to(1, band - 1).start()

    @pl.when(jnp.logical_not(first))
    def _():
        rows_to(1, band - 1).wait_send()
        pltpu.make_async_copy(caps.at[0], caps.at[0], halo_recv.at[2]).wait()

    @pl.when(jnp.logical_not(last))
    def _():
        rows_to(0, band + 1).wait_send()
        pltpu.make_async_copy(caps.at[1], caps.at[1], halo_recv.at[3]).wait()

    through = pltpu.make_async_copy(work, out, local_sem.at[1])

    def send_chunk(chunk):
        for step in range(parts):
            there = lax.rem(part + step, parts)
            pltpu.make_async_remote_copy(
                src_ref=block(work, there + parts, chunk),
                dst_ref=circles.at[chunk, part],
                send_sem=send_sem.at[chunk, there + parts],
                recv_sem=recv_sem.at[chunk, part],
                device_id=(there, helper),
                device_id_type=MESH,
            ).start()
            if step == 0:
                pltpu.make_async_copy(
                    block(work, me, chunk), circles.at[chunk, part], recv_sem.at[chunk, part]
                ).start()
            else:
                pltpu.make_async_remote_copy(
                    src_ref=block(work, there, chunk),
                    dst_ref=circles.at[chunk, part],
                    send_sem=send_sem.at[chunk, there],
                    recv_sem=recv_sem.at[chunk, part],
                    device_id=(there, band),
                    device_id_type=MESH,
                ).start()

    span = 2 * per
    for begin in range(0, levels, span):
        for level in range(begin, begin + span):
            substep_level(state, ring, caps, courant, field, work, level, first, last)

        @pl.when(polar)
        def _():
            @pl.loop(begin // span * row_chunks, (begin // span + 1) * row_chunks)
            def _(chunk):
                send_chunk(chunk)

    @pl.when(jnp.logical_not(polar))
    def _():
        through.start()

    cos1, sin1, cos2, sin2 = (twists[i : i + 1, :] for i in range(4))
    half, whole = rows, per * rows

    @pl.loop(0, chunks)
    def _(chunk):
        for i in range(parts):
            slot = circles.at[chunk, i]
            pltpu.make_async_copy(slot, slot, recv_sem.at[chunk, i]).wait()
        q0, q1, q2, q3 = (circles[chunk, i].reshape(whole, quarter) for i in range(4))
        sum_a, sum_b, odd_a, odd_b = q0 + q2, q1 + q3, q0 - q2, q1 - q3
        skew = sum_a - sum_b
        skew_a, skew_b = skew[:half], skew[half:]
        stack = jnp.concatenate(
            [
                sum_a + sum_b,
                skew_a * cos2 + skew_b * sin2,
                skew_b * cos2 - skew_a * sin2,
                odd_a * cos1 - odd_b * sin1,
                -odd_a * sin1 - odd_b * cos1,
            ],
            axis=0,
        )
        split_store(operand, stack)
        product(operand, high, low, waves, False)
        row = pl.multiple_of((chunk % row_chunks) * rows, rows)
        g = [gains[i, pl.ds(row, rows), :] for i in range(5)]
        same0, same2, cross2, same1, cross1 = (
            g[0], g[1], g[2], jnp.concatenate([g[3]] * per), jnp.concatenate([g[4]] * per)
        )
        same0 = jnp.concatenate([same0] * per)
        cos_part, sin_part = waves[:, :lanes], waves[:, lanes:]
        two_a, two_b = slice(whole, whole + half), slice(whole + half, 2 * whole)
        one_a, one_b = slice(2 * whole, 3 * whole), slice(3 * whole, 4 * whole)
        rc2, rs2, ic2, is2 = mix(
            cos_part[two_a], sin_part[two_a], cos_part[two_b], sin_part[two_b], same2, cross2
        )
        rc1, rs1, ic1, is1 = mix(
            cos_part[one_a], sin_part[one_a], cos_part[one_b], sin_part[one_b], same1, cross1
        )
        damped = jnp.concatenate(
            [
                jnp.concatenate([same0 * cos_part[:whole], rc2, ic2, rc1, ic1], axis=0),
                jnp.concatenate([same0 * sin_part[:whole], rs2, is2, rs1, is1], axis=0),
            ],
            axis=1,
        )
        split_store(operand, damped)
        product(operand, high, low, waves, True)
        back = waves[:, :quarter]
        even, two_real, two_imag = back[:whole], back[two_a], back[two_b]
        one_real, one_imag = back[one_a], back[one_b]
        odd_a = one_real * cos1 - one_imag * sin1
        odd_b = -one_real * sin1 - one_imag * cos1
        skew = jnp.concatenate(
            [two_real * cos2 - two_imag * sin2, two_imag * cos2 + two_real * sin2], axis=0
        )
        plus, minus = even + skew, even - skew
        shape = (per, rows, quarter)
        results[chunk, 0] = (plus + odd_a).reshape(shape)
        results[chunk, 1] = (minus + odd_b).reshape(shape)
        results[chunk, 2] = (plus - odd_a).reshape(shape)
        results[chunk, 3] = (minus - odd_b).reshape(shape)
        if quarter < width:
            operand[:, quarter:] = jnp.zeros_like(operand[:, quarter:])
        for step in range(1, parts):
            there = lax.rem(part + step, parts)
            pltpu.make_async_remote_copy(
                src_ref=results.at[chunk, there],
                dst_ref=block(out, me, chunk),
                send_sem=back_send_sem.at[chunk, there],
                recv_sem=back_recv_sem.at[chunk, me],
                device_id=(there, source),
                device_id_type=MESH,
            ).start()

        @pl.when(polar)
        def _():
            pltpu.make_async_copy(
                results.at[chunk, part], block(out, me, chunk), back_recv_sem.at[chunk, me]
            ).start()

        @pl.when(jnp.logical_not(polar))
        def _():
            pltpu.make_async_remote_copy(
                src_ref=results.at[chunk, part],
                dst_ref=block(out, me, chunk),
                send_sem=back_send_sem.at[chunk, part],
                recv_sem=back_recv_sem.at[chunk, me],
                device_id=(part, source),
                device_id_type=MESH,
            ).start()

    def drain(ref, semaphore):
        pltpu.make_async_copy(ref, ref, semaphore).wait()

    @pl.loop(0, chunks)
    def _(chunk):
        for step in range(1, parts):
            there = lax.rem(part + step, parts)
            drain(results.at[chunk, there], back_send_sem.at[chunk, there])

        @pl.when(jnp.logical_not(polar))
        def _():
            drain(results.at[chunk, part], back_send_sem.at[chunk, part])

        @pl.when(polar)
        def _():
            for step in range(parts):
                there = lax.rem(part + step, parts)
                drain(block(work, there + parts, chunk), send_sem.at[chunk, there + parts])
                drain(block(out, there + parts, chunk), back_recv_sem.at[chunk, there + parts])
                drain(block(out, there, chunk), back_recv_sem.at[chunk, there])
                if step > 0:
                    drain(block(work, there, chunk), send_sem.at[chunk, there])

    @pl.when(jnp.logical_not(polar))
    def _():
        through.wait()


def shared_substep(state, courant, cutoff):
    parts, bands = lax.axis_size("lon"), lax.axis_size("lat")
    components, levels, rows_here, quarter = state.shape
    per, rows = 2, 16
    chunks = (components * levels // (2 * parts) // per) * (rows_here // rows)
    basis = quarter_basis(quarter)
    width = basis.shape[1]
    square = np.zeros((width, width), np.float32)
    square[:quarter] = basis
    cos_twist, sin_twist = quarter_twists(quarter)
    twists = jnp.asarray(np.stack([cos_twist[0], sin_twist[0], cos_twist[1], sin_twist[1]]))
    _, source, _ = worker_group(lax.axis_index("lat"), bands)
    row_cutoff = lax.dynamic_slice_in_dim(cutoff, source * rows_here, rows_here)
    same0, two, one = damping_tables(row_cutoff, quarter)
    gains = jnp.stack([same0, *two, *one])
    vmem, anywhere = pl.BlockSpec(memory_space=pltpu.VMEM), pl.BlockSpec(memory_space=pl.ANY)
    table = pltpu.VMEM((width, width), jnp.bfloat16)
    piece = pltpu.VMEM((chunks, parts, per, rows, quarter), jnp.float32)
    lines = 4 * per * rows
    pairs = 2 * components * levels
    return pl.pallas_call(
        functools.partial(circle_kernel, bands, parts, chunks),
        out_shape=jax.ShapeDtypeStruct(state.shape, jnp.float32),
        in_specs=[vmem, vmem, vmem, vmem, anywhere],
        out_specs=anywhere,
        scratch_shapes=[
            piece,
            piece,
            pltpu.VMEM((width, width), jnp.float32),
            table,
            table,
            pltpu.VMEM((2 * lines, width), jnp.bfloat16),
            pltpu.VMEM((lines, width), jnp.float32),
            pltpu.VMEM((components, levels, rows_here, 128), jnp.float32),
            pltpu.VMEM((2, components, levels, rows_here, 128), jnp.float32),
            pltpu.VMEM((2, pairs, width), jnp.float32),
            pltpu.VMEM((2, pairs, width), jnp.float32),
            pltpu.VMEM((components, rows_here + 16, width), jnp.float32),
            pltpu.VMEM(state.shape, jnp.float32),
            pltpu.SemaphoreType.DMA((chunks, 2 * parts)),
            pltpu.SemaphoreType.DMA((chunks, parts)),
            pltpu.SemaphoreType.DMA((chunks, parts)),
            pltpu.SemaphoreType.DMA((chunks, 2 * parts)),
            pltpu.SemaphoreType.DMA((2,)),
            pltpu.SemaphoreType.DMA((4,)),
            pltpu.SemaphoreType.DMA((4,)),
        ],
        compiler_params=pltpu.CompilerParams(
            collective_id=0, has_side_effects=True, vmem_limit_bytes=56 * 2**20
        ),
    )(state, courant[:, None], gains, twists, jnp.asarray(square))


def fits_shared(state):
    parts, bands = lax.axis_size("lon"), lax.axis_size("lat")
    components, levels, rows_here, quarter = state.shape
    return (
        parts == 4
        and components == parts
        and bands % 4 == 0
        and levels % 4 == 0
        and rows_here % 16 == 0
        and quarter % 128 == 32
    )


def per_device(model_state, courant, cutoff):
    if fits_shared(model_state):
        return shared_substep(model_state, courant, cutoff)
    rows_here = model_state.shape[2]
    band_index = lax.axis_index("lat")
    extended = with_halo(model_state, (("lon", 3), ("lat", 2)), 1)
    extended = trim_rims(extended, 2)
    wind_east = extended[0]
    wind_north = extended[1]
    theta_ext = extended[2]
    thickness = extended[3]
    row_courant = courant[None, :, None]
    east_flux = wind_east * thickness
    north_flux = wind_north * thickness
    heat_content = theta_ext * thickness
    new_thickness = (
        thickness[:, 1:-1, 1:-1]
        - row_courant * along_lon(east_flux)
        - meridional_courant * along_lat(north_flux)
    )
    new_heat = (
        heat_content[:, 1:-1, 1:-1]
        - row_courant * along_lon(east_flux * theta_ext)
        - meridional_courant * along_lat(north_flux * theta_ext)
    )
    new_theta = new_heat / new_thickness
    heat_ext = trim_rims(with_halo(new_heat, (("lon", 2), ("lat", 1)), 1), 1)
    new_east = wind_east[:, 1:-1, 1:-1] - pressure_gain * row_courant * along_lon(heat_ext)
    new_north = wind_north[:, 1:-1, 1:-1] - pressure_gain * meridional_courant * along_lat(heat_ext)
    stacked = jnp.stack([new_east, new_north, new_theta, new_thickness])
    own_cut = lax.dynamic_slice_in_dim(cutoff, band_index * rows_here, rows_here)
    return filter_block(stacked, own_cut)


def solution(mesh):
    placed = (P(None, None, "lat", "lon"), P("lat"), P())
    return jax.shard_map(
        per_device,
        mesh=mesh,
        in_specs=placed,
        out_specs=P(None, None, "lat", "lon"),
        check_vma=False,
    )
```

```python
import functools

import jax
import jax.numpy as jnp
import numpy as np
from jax import lax
from jax.experimental import pallas as pl
from jax.experimental.pallas import tpu as pltpu
from jax.sharding import PartitionSpec as P

meridional_courant = 0.05
pressure_gain = 4.0
courant_lane = 64
MESH = pl.DeviceIdType.MESH


def with_halo(array, sides, width):
    for axis, dim in sides:
        size, length = (lax.axis_size(axis), array.shape[dim])
        up = [(i, (i + 1) % size) for i in range(size)]
        down = [(j, i) for i, j in up]
        last = lax.slice_in_dim(array, length - width, length, axis=dim)
        first = lax.slice_in_dim(array, 0, width, axis=dim)
        before = lax.ppermute(last, axis, up)
        after = lax.ppermute(first, axis, down)
        array = jnp.concatenate([before, array, after], axis=dim)
    return array


def quarter_basis(quarter):
    half = quarter // 2
    lanes = -(-(half + 1) // 128) * 128
    phase = np.outer(np.arange(quarter), np.arange(half + 1)) % quarter
    angle = 2.0 * np.pi / quarter * phase
    table = np.zeros((quarter, 2 * lanes), np.float32)
    table[:, : half + 1] = np.cos(angle)
    table[:, lanes : lanes + half + 1] = np.sin(angle)
    return table


def quarter_twists(quarter):
    angle = 2.0 * np.pi / (4 * quarter) * np.outer([1.0, 2.0], np.arange(quarter))
    return np.cos(angle).astype(np.float32), np.sin(angle).astype(np.float32)


def damping_tables(row_cutoff, quarter):
    half = quarter // 2
    length = 4 * quarter
    lanes = -(-(half + 1) // 128) * 128
    index = jnp.arange(lanes, dtype=jnp.int32)
    inside = index <= half
    weight = jnp.where(inside, jnp.where((index == 0) | (index == half), 1.0, 2.0), 0.0) / quarter
    cut = row_cutoff.astype(jnp.float32)[:, None]

    def damping(wave_number):
        wave_number = jnp.abs(wave_number)
        folded = jnp.minimum(wave_number, length - wave_number)
        ratio = cut / jnp.maximum(folded, 1).astype(jnp.float32)[None, :]
        return jnp.minimum(1.0, ratio * ratio)

    def pair(shift, scale):
        above = damping(4 * index + shift)
        below = damping(4 * index - shift)
        gain = weight[None, :] * (0.5 * scale)
        return gain * (above + below), gain * (above - below)

    return pair(0, 0.25)[0], pair(2, 0.25), pair(1, 0.5)


def mix(real_cos, real_sin, imag_cos, imag_sin, same, cross):
    return (
        same * real_cos + cross * imag_sin,
        same * real_sin - cross * imag_cos,
        same * imag_cos - cross * real_sin,
        same * imag_sin + cross * real_cos,
    )


def damp_quarters(quarters, row_cutoff):
    _, planes, rows, quarter = quarters.shape
    basis = jnp.asarray(quarter_basis(quarter))
    cos_twist, sin_twist = quarter_twists(quarter)
    q0, q1, q2, q3 = quarters
    even, odd_a, odd_b = (q0 + q2) + (q1 + q3), q0 - q2, q1 - q3
    skew = (q0 + q2) - (q1 + q3)
    pairs = planes // 2
    skew_a, skew_b = skew[:pairs], skew[pairs:]
    one_real = odd_a * cos_twist[0] - odd_b * sin_twist[0]
    one_imag = -odd_a * sin_twist[0] - odd_b * cos_twist[0]
    two_real = skew_a * cos_twist[1] + skew_b * sin_twist[1]
    two_imag = skew_b * cos_twist[1] - skew_a * sin_twist[1]
    stack = jnp.concatenate([even, two_real, two_imag, one_real, one_imag], axis=0)
    waves = jnp.einsum("prm,mk->prk", stack, basis, precision=lax.Precision.HIGH)
    lanes = basis.shape[1] // 2
    cos_part, sin_part = waves[..., :lanes], waves[..., lanes:]
    same0, (same2, cross2), (same1, cross1) = damping_tables(row_cutoff, quarter)
    p, h = planes, pairs
    two = slice(p, p + h), slice(p + h, 2 * p)
    one = slice(2 * p, 3 * p), slice(3 * p, 4 * p)
    even_c, even_s = same0 * cos_part[:p], same0 * sin_part[:p]
    rc2, rs2, ic2, is2 = mix(
        cos_part[two[0]], sin_part[two[0]], cos_part[two[1]], sin_part[two[1]], same2, cross2
    )
    rc1, rs1, ic1, is1 = mix(
        cos_part[one[0]], sin_part[one[0]], cos_part[one[1]], sin_part[one[1]], same1, cross1
    )
    damped = jnp.concatenate(
        [
            jnp.concatenate([even_c, rc2, ic2, rc1, ic1], axis=0),
            jnp.concatenate([even_s, rs2, is2, rs1, is1], axis=0),
        ],
        axis=-1,
    )
    back = jnp.einsum("prk,mk->prm", damped, basis, precision=lax.Precision.HIGH)
    even, two_real, two_imag = back[:p], back[two[0]], back[two[1]]
    one_real, one_imag = back[one[0]], back[one[1]]
    odd_a = one_real * cos_twist[0] - one_imag * sin_twist[0]
    odd_b = -one_real * sin_twist[0] - one_imag * cos_twist[0]
    skew = jnp.concatenate(
        [
            two_real * cos_twist[1] - two_imag * sin_twist[1],
            two_imag * cos_twist[1] + two_real * sin_twist[1],
        ],
        axis=0,
    )
    plus, minus = even + skew, even - skew
    return jnp.stack([plus + odd_a, minus + odd_b, plus - odd_a, minus - odd_b])


def trim_rims(extended, row_dim):
    band_index = lax.axis_index("lat")
    band_count = lax.axis_size("lat")
    rows_ext = extended.shape[row_dim]
    positions = jnp.arange(rows_ext, dtype=jnp.int32)
    keep_rows = jnp.logical_not(
        (positions == 0) & (band_index == 0)
        | (positions == rows_ext - 1) & (band_index == band_count - 1)
    )
    mask_shape = [1] * extended.ndim
    mask_shape[row_dim] = rows_ext
    return extended * keep_rows.astype(extended.dtype).reshape(mask_shape)


def along_lon(field_ext):
    return (field_ext[..., 1:-1, 2:] - field_ext[..., 1:-1, :-2]) * 0.5


def along_lat(field_ext):
    return (field_ext[..., 2:, 1:-1] - field_ext[..., :-2, 1:-1]) * 0.5


def filter_block(work_block, block_cutoff):
    lon_parts = lax.axis_size("lon")
    components, levels, rows_here, width_here = work_block.shape
    planes = components * levels // lon_parts
    group = lon_parts // 4
    lines = work_block.reshape(lon_parts, planes, rows_here, width_here)
    circles = lax.all_to_all(lines, "lon", split_axis=0, concat_axis=0, tiled=True)
    quarters = circles.reshape(4, group, planes, rows_here, width_here)
    quarters = jnp.moveaxis(quarters, 1, 3).reshape(4, planes, rows_here, group * width_here)
    smoothed = damp_quarters(quarters, block_cutoff)
    smoothed = smoothed.reshape(4, planes, rows_here, group, width_here)
    smoothed = jnp.moveaxis(smoothed, 3, 1).reshape(lines.shape)
    returned = lax.all_to_all(smoothed, "lon", split_axis=0, concat_axis=0, tiled=True)
    return returned.reshape(work_block.shape)


def worker_group(band, bands):
    quarter = bands // 4
    low = band < bands // 2
    polar = jnp.logical_or(band < quarter, band >= bands - quarter)
    inner = jnp.where(low, band - quarter, band + quarter)
    source = jnp.where(polar, band, inner)
    helper = jnp.where(source < bands // 2, source + quarter, source - quarter)
    return polar, source, helper


def split_store(ref, values):
    rows, width = values.shape
    high = values.astype(jnp.bfloat16)
    low = (values - high.astype(jnp.float32)).astype(jnp.bfloat16)
    ref[:rows, :width] = high
    ref[rows:, :width] = low


def product(parts, high_ref, low_ref, out_ref, back):
    rows = out_ref.shape[0]
    dims = (((1,), (1 if back else 0,)), ((), ()))
    for start in range(0, out_ref.shape[1], 256):
        cols = slice(start, start + 256)
        piece = (cols, slice(None)) if back else (slice(None), cols)
        both = lax.dot_general(parts[...], high_ref[piece], dims, preferred_element_type=jnp.float32)
        cross = lax.dot_general(
            parts[:rows, :], low_ref[piece], dims, preferred_element_type=jnp.float32
        )
        out_ref[:, cols] = (both[:rows] + both[rows:]) + cross


def edge_tile(state, ring, courant, component, level, rows):
    rest = state.shape[3] % 128
    tail = state[component, level, rows, state.shape[3] - rest :]
    count = tail.shape[0]
    tail = jnp.concatenate([tail, jnp.zeros((count, 128 - rest), jnp.float32)], axis=1)
    lane = lax.broadcasted_iota(jnp.int32, (count, 128), 1)
    tile = jnp.where(lane == courant_lane, courant[rows, :], tail)
    tile = jnp.where((lane == rest) | (lane == rest + 1), ring[1, component, level, rows, :], tile)
    return jnp.where(lane >= 126, ring[0, component, level, rows, :], tile)


def substep_level(state, ring, caps, courant, field, work, level, first, last):
    components, levels, rows, quarter = state.shape
    width = field.shape[2]
    body = width - 128
    for c in range(components):
        field[c, 8 : 8 + rows, :body] = state[c, level, :, :body]
        field[c, 8 : 8 + rows, body:] = edge_tile(state, ring, courant, c, level, slice(0, rows))
        field[c, 6:8, :] = caps[0, 2 * (c * levels + level) : 2 * (c * levels + level) + 2, :]
        field[c, 8 + rows : 10 + rows, :] = caps[1, 2 * (c * levels + level) : 2 * (c * levels + level) + 2, :]
    east, north, theta, thick = (field[c] for c in range(4))
    height = east.shape[0]
    row_courant = east[:, body + courant_lane : body + courant_lane + 1]

    def along_x(f):
        return (pltpu.roll(f, width - 1, 1) - pltpu.roll(f, 1, 1)) * 0.5

    def along_y(f):
        return (pltpu.roll(f, height - 1, 0) - pltpu.roll(f, 1, 0)) * 0.5

    east_flux, north_flux = east * thick, north * thick
    new_thick = thick - row_courant * along_x(east_flux) - meridional_courant * along_y(north_flux)
    heat = (
        theta * thick
        - row_courant * along_x(east_flux * theta)
        - meridional_courant * along_y(north_flux * theta)
    )
    row = lax.broadcasted_iota(jnp.int32, (height, 1), 0)
    beyond = (first & (row < 8)) | (last & (row >= 8 + rows))
    heat = jnp.where(beyond, 0.0, heat)
    new_east = east - pressure_gain * row_courant * along_x(heat)
    new_north = north - pressure_gain * meridional_courant * along_y(heat)
    own = slice(8, 8 + rows)
    work[0, level] = new_east[own, :quarter]
    work[1, level] = new_north[own, :quarter]
    work[2, level] = heat[own, :quarter] / new_thick[own, :quarter]
    work[3, level] = new_thick[own, :quarter]


def circle_kernel(
    bands, parts, chunks, state, courant, gains, twists, table, out, circles, results, basis, high, low,
    operand, waves, pack, ring, edges, caps, field, work, relay,
    send_sem, recv_sem, back_send_sem, back_recv_sem, local_sem, halo_send, halo_recv,
    relay_send, relay_recv,
):
    part = lax.axis_index("lon")
    band = lax.axis_index("lat")
    polar, source, helper = worker_group(band, bands)
    _, _, per, rows, quarter = circles.shape
    components, levels, rows_here, _ = state.shape
    width = high.shape[1]
    lanes = width // 2
    row_chunks = rows_here // rows
    me = jnp.where(polar, part, part + parts)
    first, last = band == 0, band == bands - 1

    def block(ref, worker, chunk):
        level = (chunk // row_chunks) * 2 * per + (worker // parts) * per
        row = pl.multiple_of((chunk % row_chunks) * rows, rows)
        return ref.at[lax.rem(worker, parts), pl.ds(level, per), pl.ds(row, rows), :]

    load = pltpu.make_async_copy(table, basis, local_sem.at[0])
    load.start()

    caps[...] = jnp.zeros_like(caps)
    barrier = pltpu.get_barrier_semaphore()

    def greet(there, row_band):
        pl.semaphore_signal(barrier, inc=1, device_id=(there, row_band), device_id_type=MESH)

    for step in range(1, parts):
        greet(lax.rem(part + step, parts), band)
    for step in range(parts):
        greet(lax.rem(part + step, parts), jnp.where(polar, helper, source))

    @pl.when(band > 0)
    def _():
        greet(part, band - 1)

    @pl.when(band < bands - 1)
    def _():
        greet(part, band + 1)

    rest = quarter % 128
    lane = lax.broadcasted_iota(jnp.int32, (rows_here, 128), 1)

    @pl.loop(0, levels)
    def _(level):
        for c in range(components):
            begin = pltpu.roll(state[c, level, :, :128], rest, 1)
            tail = state[c, level, :, quarter - rest :]
            tail = jnp.concatenate([tail, jnp.zeros((rows_here, 128 - rest), jnp.float32)], axis=1)
            pack[c, level] = jnp.where(lane >= 126, pltpu.roll(tail, 128 - rest, 1), begin)

    inner_bands = jnp.where(first | last, 1, 2)
    pl.semaphore_wait(barrier, 2 * parts - 1 + inner_bands)
    columns = [
        pltpu.make_async_remote_copy(
            src_ref=pack,
            dst_ref=ring.at[slot],
            send_sem=halo_send.at[slot],
            recv_sem=halo_recv.at[slot],
            device_id=(lax.rem(part + shift, parts), band),
            device_id_type=MESH,
        )
        for slot, shift in ((0, 1), (1, parts - 1))
    ]
    for copy in columns:
        copy.start()
    field[...] = jnp.zeros_like(field)
    operand[...] = jnp.zeros_like(operand)
    load.wait()

    @pl.loop(0, width // 32)
    def _(step):
        at = pl.ds(pl.multiple_of(step * 32, 32), 32)
        exact = basis[at, :]
        upper = exact.astype(jnp.bfloat16)
        high[at, :] = upper
        low[at, :] = (exact - upper.astype(jnp.float32)).astype(jnp.bfloat16)

    for copy in columns:
        copy.wait()

    body = width - 128
    for c in range(components):
        for level in range(levels):
            at = slice(2 * (c * levels + level), 2 * (c * levels + level) + 2)
            for slot, own in ((0, slice(rows_here - 2, rows_here)), (1, slice(0, 2))):
                edges[slot, at, :body] = state[c, level, own, :body]
                edges[slot, at, body:] = edge_tile(state, ring, courant, c, level, own)

    def rows_to(slot, row_band):
        return pltpu.make_async_remote_copy(
            src_ref=edges.at[slot],
            dst_ref=caps.at[slot],
            send_sem=halo_send.at[2 + slot],
            recv_sem=halo_recv.at[2 + slot],
            device_id=(part, row_band),
            device_id_type=MESH,
        )

    @pl.when(jnp.logical_not(last))
    def _():
        rows_to(0, band + 1).start()

    @pl.when(jnp.logical_not(first))
    def _():
        rows_to(1, band - 1).start()

    @pl.when(jnp.logical_not(first))
    def _():
        rows_to(1, band - 1).wait_send()
        pltpu.make_async_copy(caps.at[0], caps.at[0], halo_recv.at[2]).wait()

    @pl.when(jnp.logical_not(last))
    def _():
        rows_to(0, band + 1).wait_send()
        pltpu.make_async_copy(caps.at[1], caps.at[1], halo_recv.at[3]).wait()

    through = pltpu.make_async_copy(work, out, local_sem.at[1])

    sibling = part + 1 - 2 * lax.rem(part, 2)
    far = (lax.rem(part + 2, parts), lax.rem(sibling + 2, parts))

    def send_chunk(chunk):
        def send(worker, target, target_band, slot, semaphore):
            pltpu.make_async_remote_copy(
                src_ref=block(work, worker, chunk),
                dst_ref=slot,
                send_sem=send_sem.at[chunk, worker],
                recv_sem=semaphore,
                device_id=(target, target_band),
                device_id_type=MESH,
            ).start()

        here, landed = circles.at[chunk, part], recv_sem.at[chunk, part]
        for i, there in enumerate(far):
            send(there + parts, part, helper, relay.at[chunk, i], relay_recv.at[chunk, i])
            send(there, there, band, here, landed)
        for there in (sibling, part):
            send(there + parts, there, helper, here, landed)
        send(sibling, sibling, band, here, landed)
        pltpu.make_async_copy(block(work, me, chunk), here, landed).start()

    span = 2 * per
    for begin in range(0, levels, span):
        for level in range(begin, begin + span):
            substep_level(state, ring, caps, courant, field, work, level, first, last)

        @pl.when(polar)
        def _():
            @pl.loop(begin // span * row_chunks, (begin // span + 1) * row_chunks)
            def _(chunk):
                send_chunk(chunk)

    @pl.when(jnp.logical_not(polar))
    def _():
        through.start()

    cos1, sin1, cos2, sin2 = (twists[i : i + 1, :] for i in range(4))
    half, whole = rows, per * rows

    @pl.loop(0, chunks)
    def _(chunk):
        @pl.when(jnp.logical_not(polar))
        def _():
            for i, there in enumerate(far):
                slot = relay.at[chunk, i]
                pltpu.make_async_copy(slot, slot, relay_recv.at[chunk, i]).wait()
                pltpu.make_async_remote_copy(
                    src_ref=slot,
                    dst_ref=circles.at[chunk, part],
                    send_sem=relay_send.at[chunk, i],
                    recv_sem=recv_sem.at[chunk, part],
                    device_id=(there, band),
                    device_id_type=MESH,
                ).start()

        for i in range(parts):
            slot = circles.at[chunk, i]
            pltpu.make_async_copy(slot, slot, recv_sem.at[chunk, i]).wait()
        q0, q1, q2, q3 = (circles[chunk, i].reshape(whole, quarter) for i in range(4))
        sum_a, sum_b, odd_a, odd_b = q0 + q2, q1 + q3, q0 - q2, q1 - q3
        skew = sum_a - sum_b
        skew_a, skew_b = skew[:half], skew[half:]
        stack = jnp.concatenate(
            [
                sum_a + sum_b,
                skew_a * cos2 + skew_b * sin2,
                skew_b * cos2 - skew_a * sin2,
                odd_a * cos1 - odd_b * sin1,
                -odd_a * sin1 - odd_b * cos1,
            ],
            axis=0,
        )
        split_store(operand, stack)
        product(operand, high, low, waves, False)
        row = pl.multiple_of((chunk % row_chunks) * rows, rows)
        g = [gains[i, pl.ds(row, rows), :] for i in range(5)]
        same0, same2, cross2, same1, cross1 = (
            g[0], g[1], g[2], jnp.concatenate([g[3]] * per), jnp.concatenate([g[4]] * per)
        )
        same0 = jnp.concatenate([same0] * per)
        cos_part, sin_part = waves[:, :lanes], waves[:, lanes:]
        two_a, two_b = slice(whole, whole + half), slice(whole + half, 2 * whole)
        one_a, one_b = slice(2 * whole, 3 * whole), slice(3 * whole, 4 * whole)
        rc2, rs2, ic2, is2 = mix(
            cos_part[two_a], sin_part[two_a], cos_part[two_b], sin_part[two_b], same2, cross2
        )
        rc1, rs1, ic1, is1 = mix(
            cos_part[one_a], sin_part[one_a], cos_part[one_b], sin_part[one_b], same1, cross1
        )
        damped = jnp.concatenate(
            [
                jnp.concatenate([same0 * cos_part[:whole], rc2, ic2, rc1, ic1], axis=0),
                jnp.concatenate([same0 * sin_part[:whole], rs2, is2, rs1, is1], axis=0),
            ],
            axis=1,
        )
        split_store(operand, damped)
        product(operand, high, low, waves, True)
        back = waves[:, :quarter]
        even, two_real, two_imag = back[:whole], back[two_a], back[two_b]
        one_real, one_imag = back[one_a], back[one_b]
        odd_a = one_real * cos1 - one_imag * sin1
        odd_b = -one_real * sin1 - one_imag * cos1
        skew = jnp.concatenate(
            [two_real * cos2 - two_imag * sin2, two_imag * cos2 + two_real * sin2], axis=0
        )
        plus, minus = even + skew, even - skew
        shape = (per, rows, quarter)
        results[chunk, 0] = (plus + odd_a).reshape(shape)
        results[chunk, 1] = (minus + odd_b).reshape(shape)
        results[chunk, 2] = (plus - odd_a).reshape(shape)
        results[chunk, 3] = (minus - odd_b).reshape(shape)
        if quarter < width:
            operand[:, quarter:] = jnp.zeros_like(operand[:, quarter:])
        for step in range(1, parts):
            there = lax.rem(part + step, parts)
            pltpu.make_async_remote_copy(
                src_ref=results.at[chunk, there],
                dst_ref=block(out, me, chunk),
                send_sem=back_send_sem.at[chunk, there],
                recv_sem=back_recv_sem.at[chunk, me],
                device_id=(there, source),
                device_id_type=MESH,
            ).start()

        @pl.when(polar)
        def _():
            pltpu.make_async_copy(
                results.at[chunk, part], block(out, me, chunk), back_recv_sem.at[chunk, me]
            ).start()

        @pl.when(jnp.logical_not(polar))
        def _():
            pltpu.make_async_remote_copy(
                src_ref=results.at[chunk, part],
                dst_ref=block(out, me, chunk),
                send_sem=back_send_sem.at[chunk, part],
                recv_sem=back_recv_sem.at[chunk, me],
                device_id=(part, source),
                device_id_type=MESH,
            ).start()

    def drain(ref, semaphore):
        pltpu.make_async_copy(ref, ref, semaphore).wait()

    @pl.loop(0, chunks)
    def _(chunk):
        for step in range(1, parts):
            there = lax.rem(part + step, parts)
            drain(results.at[chunk, there], back_send_sem.at[chunk, there])

        @pl.when(jnp.logical_not(polar))
        def _():
            drain(results.at[chunk, part], back_send_sem.at[chunk, part])
            for i in range(2):
                drain(relay.at[chunk, i], relay_send.at[chunk, i])

        @pl.when(polar)
        def _():
            for step in range(parts):
                there = lax.rem(part + step, parts)
                drain(block(work, there + parts, chunk), send_sem.at[chunk, there + parts])
                drain(block(out, there + parts, chunk), back_recv_sem.at[chunk, there + parts])
                drain(block(out, there, chunk), back_recv_sem.at[chunk, there])
                if step > 0:
                    drain(block(work, there, chunk), send_sem.at[chunk, there])

    @pl.when(jnp.logical_not(polar))
    def _():
        through.wait()


def shared_substep(state, courant, cutoff):
    parts, bands = lax.axis_size("lon"), lax.axis_size("lat")
    components, levels, rows_here, quarter = state.shape
    per, rows = 2, 16
    chunks = (components * levels // (2 * parts) // per) * (rows_here // rows)
    basis = quarter_basis(quarter)
    width = basis.shape[1]
    square = np.zeros((width, width), np.float32)
    square[:quarter] = basis
    cos_twist, sin_twist = quarter_twists(quarter)
    twists = jnp.asarray(np.stack([cos_twist[0], sin_twist[0], cos_twist[1], sin_twist[1]]))
    _, source, _ = worker_group(lax.axis_index("lat"), bands)
    row_cutoff = lax.dynamic_slice_in_dim(cutoff, source * rows_here, rows_here)
    same0, two, one = damping_tables(row_cutoff, quarter)
    gains = jnp.stack([same0, *two, *one])
    vmem, anywhere = pl.BlockSpec(memory_space=pltpu.VMEM), pl.BlockSpec(memory_space=pl.ANY)
    table = pltpu.VMEM((width, width), jnp.bfloat16)
    piece = pltpu.VMEM((chunks, parts, per, rows, quarter), jnp.float32)
    lines = 4 * per * rows
    pairs = 2 * components * levels
    return pl.pallas_call(
        functools.partial(circle_kernel, bands, parts, chunks),
        out_shape=jax.ShapeDtypeStruct(state.shape, jnp.float32),
        in_specs=[vmem, vmem, vmem, vmem, anywhere],
        out_specs=anywhere,
        scratch_shapes=[
            piece,
            piece,
            pltpu.VMEM((width, width), jnp.float32),
            table,
            table,
            pltpu.VMEM((2 * lines, width), jnp.bfloat16),
            pltpu.VMEM((lines, width), jnp.float32),
            pltpu.VMEM((components, levels, rows_here, 128), jnp.float32),
            pltpu.VMEM((2, components, levels, rows_here, 128), jnp.float32),
            pltpu.VMEM((2, pairs, width), jnp.float32),
            pltpu.VMEM((2, pairs, width), jnp.float32),
            pltpu.VMEM((components, rows_here + 16, width), jnp.float32),
            pltpu.VMEM(state.shape, jnp.float32),
            pltpu.VMEM((chunks, 2, per, rows, quarter), jnp.float32),
            pltpu.SemaphoreType.DMA((chunks, 2 * parts)),
            pltpu.SemaphoreType.DMA((chunks, parts)),
            pltpu.SemaphoreType.DMA((chunks, parts)),
            pltpu.SemaphoreType.DMA((chunks, 2 * parts)),
            pltpu.SemaphoreType.DMA((2,)),
            pltpu.SemaphoreType.DMA((4,)),
            pltpu.SemaphoreType.DMA((4,)),
            pltpu.SemaphoreType.DMA((chunks, 2)),
            pltpu.SemaphoreType.DMA((chunks, 2)),
        ],
        compiler_params=pltpu.CompilerParams(
            collective_id=0, has_side_effects=True, vmem_limit_bytes=56 * 2**20
        ),
    )(state, courant[:, None], gains, twists, jnp.asarray(square))


def fits_shared(state):
    parts, bands = lax.axis_size("lon"), lax.axis_size("lat")
    components, levels, rows_here, quarter = state.shape
    return (
        parts == 4
        and components == parts
        and bands % 4 == 0
        and levels % 4 == 0
        and rows_here % 16 == 0
        and quarter % 128 == 32
    )


def per_device(model_state, courant, cutoff):
    if fits_shared(model_state):
        return shared_substep(model_state, courant, cutoff)
    rows_here = model_state.shape[2]
    band_index = lax.axis_index("lat")
    extended = with_halo(model_state, (("lon", 3), ("lat", 2)), 1)
    extended = trim_rims(extended, 2)
    wind_east = extended[0]
    wind_north = extended[1]
    theta_ext = extended[2]
    thickness = extended[3]
    row_courant = courant[None, :, None]
    east_flux = wind_east * thickness
    north_flux = wind_north * thickness
    heat_content = theta_ext * thickness
    new_thickness = (
        thickness[:, 1:-1, 1:-1]
        - row_courant * along_lon(east_flux)
        - meridional_courant * along_lat(north_flux)
    )
    new_heat = (
        heat_content[:, 1:-1, 1:-1]
        - row_courant * along_lon(east_flux * theta_ext)
        - meridional_courant * along_lat(north_flux * theta_ext)
    )
    new_theta = new_heat / new_thickness
    heat_ext = trim_rims(with_halo(new_heat, (("lon", 2), ("lat", 1)), 1), 1)
    new_east = wind_east[:, 1:-1, 1:-1] - pressure_gain * row_courant * along_lon(heat_ext)
    new_north = wind_north[:, 1:-1, 1:-1] - pressure_gain * meridional_courant * along_lat(heat_ext)
    stacked = jnp.stack([new_east, new_north, new_theta, new_thickness])
    own_cut = lax.dynamic_slice_in_dim(cutoff, band_index * rows_here, rows_here)
    return filter_block(stacked, own_cut)


def solution(mesh):
    placed = (P(None, None, "lat", "lon"), P("lat"), P())
    return jax.shard_map(
        per_device,
        mesh=mesh,
        in_specs=placed,
        out_specs=P(None, None, "lat", "lon"),
        check_vma=False,
    )
```

```python
import functools

import jax
import jax.numpy as jnp
import numpy as np
from jax import lax
from jax.experimental import pallas as pl
from jax.experimental.pallas import tpu as pltpu
from jax.sharding import PartitionSpec as P

meridional_courant = 0.05
pressure_gain = 4.0
courant_lane = 64
MESH = pl.DeviceIdType.MESH


def with_halo(array, sides, width):
    for axis, dim in sides:
        size, length = (lax.axis_size(axis), array.shape[dim])
        up = [(i, (i + 1) % size) for i in range(size)]
        down = [(j, i) for i, j in up]
        last = lax.slice_in_dim(array, length - width, length, axis=dim)
        first = lax.slice_in_dim(array, 0, width, axis=dim)
        before = lax.ppermute(last, axis, up)
        after = lax.ppermute(first, axis, down)
        array = jnp.concatenate([before, array, after], axis=dim)
    return array


def quarter_basis(quarter):
    half = quarter // 2
    lanes = -(-(half + 1) // 128) * 128
    phase = np.outer(np.arange(quarter), np.arange(half + 1)) % quarter
    angle = 2.0 * np.pi / quarter * phase
    table = np.zeros((quarter, 2 * lanes), np.float32)
    table[:, : half + 1] = np.cos(angle)
    table[:, lanes : lanes + half + 1] = np.sin(angle)
    return table


def quarter_twists(quarter):
    angle = 2.0 * np.pi / (4 * quarter) * np.outer([1.0, 2.0], np.arange(quarter))
    return np.cos(angle).astype(np.float32), np.sin(angle).astype(np.float32)


def damping_tables(row_cutoff, quarter):
    half = quarter // 2
    length = 4 * quarter
    lanes = -(-(half + 1) // 128) * 128
    index = jnp.arange(lanes, dtype=jnp.int32)
    inside = index <= half
    weight = jnp.where(inside, jnp.where((index == 0) | (index == half), 1.0, 2.0), 0.0) / quarter
    cut = row_cutoff.astype(jnp.float32)[:, None]

    def damping(wave_number):
        wave_number = jnp.abs(wave_number)
        folded = jnp.minimum(wave_number, length - wave_number)
        ratio = cut / jnp.maximum(folded, 1).astype(jnp.float32)[None, :]
        return jnp.minimum(1.0, ratio * ratio)

    def pair(shift, scale):
        above = damping(4 * index + shift)
        below = damping(4 * index - shift)
        gain = weight[None, :] * (0.5 * scale)
        return gain * (above + below), gain * (above - below)

    return pair(0, 0.25)[0], pair(2, 0.25), pair(1, 0.5)


def mix(real_cos, real_sin, imag_cos, imag_sin, same, cross):
    return (
        same * real_cos + cross * imag_sin,
        same * real_sin - cross * imag_cos,
        same * imag_cos - cross * real_sin,
        same * imag_sin + cross * real_cos,
    )


def damp_quarters(quarters, row_cutoff):
    _, planes, rows, quarter = quarters.shape
    basis = jnp.asarray(quarter_basis(quarter))
    cos_twist, sin_twist = quarter_twists(quarter)
    q0, q1, q2, q3 = quarters
    even, odd_a, odd_b = (q0 + q2) + (q1 + q3), q0 - q2, q1 - q3
    skew = (q0 + q2) - (q1 + q3)
    pairs = planes // 2
    skew_a, skew_b = skew[:pairs], skew[pairs:]
    one_real = odd_a * cos_twist[0] - odd_b * sin_twist[0]
    one_imag = -odd_a * sin_twist[0] - odd_b * cos_twist[0]
    two_real = skew_a * cos_twist[1] + skew_b * sin_twist[1]
    two_imag = skew_b * cos_twist[1] - skew_a * sin_twist[1]
    stack = jnp.concatenate([even, two_real, two_imag, one_real, one_imag], axis=0)
    waves = jnp.einsum("prm,mk->prk", stack, basis, precision=lax.Precision.HIGH)
    lanes = basis.shape[1] // 2
    cos_part, sin_part = waves[..., :lanes], waves[..., lanes:]
    same0, (same2, cross2), (same1, cross1) = damping_tables(row_cutoff, quarter)
    p, h = planes, pairs
    two = slice(p, p + h), slice(p + h, 2 * p)
    one = slice(2 * p, 3 * p), slice(3 * p, 4 * p)
    even_c, even_s = same0 * cos_part[:p], same0 * sin_part[:p]
    rc2, rs2, ic2, is2 = mix(
        cos_part[two[0]], sin_part[two[0]], cos_part[two[1]], sin_part[two[1]], same2, cross2
    )
    rc1, rs1, ic1, is1 = mix(
        cos_part[one[0]], sin_part[one[0]], cos_part[one[1]], sin_part[one[1]], same1, cross1
    )
    damped = jnp.concatenate(
        [
            jnp.concatenate([even_c, rc2, ic2, rc1, ic1], axis=0),
            jnp.concatenate([even_s, rs2, is2, rs1, is1], axis=0),
        ],
        axis=-1,
    )
    back = jnp.einsum("prk,mk->prm", damped, basis, precision=lax.Precision.HIGH)
    even, two_real, two_imag = back[:p], back[two[0]], back[two[1]]
    one_real, one_imag = back[one[0]], back[one[1]]
    odd_a = one_real * cos_twist[0] - one_imag * sin_twist[0]
    odd_b = -one_real * sin_twist[0] - one_imag * cos_twist[0]
    skew = jnp.concatenate(
        [
            two_real * cos_twist[1] - two_imag * sin_twist[1],
            two_imag * cos_twist[1] + two_real * sin_twist[1],
        ],
        axis=0,
    )
    plus, minus = even + skew, even - skew
    return jnp.stack([plus + odd_a, minus + odd_b, plus - odd_a, minus - odd_b])


def trim_rims(extended, row_dim):
    band_index = lax.axis_index("lat")
    band_count = lax.axis_size("lat")
    rows_ext = extended.shape[row_dim]
    positions = jnp.arange(rows_ext, dtype=jnp.int32)
    keep_rows = jnp.logical_not(
        (positions == 0) & (band_index == 0)
        | (positions == rows_ext - 1) & (band_index == band_count - 1)
    )
    mask_shape = [1] * extended.ndim
    mask_shape[row_dim] = rows_ext
    return extended * keep_rows.astype(extended.dtype).reshape(mask_shape)


def along_lon(field_ext):
    return (field_ext[..., 1:-1, 2:] - field_ext[..., 1:-1, :-2]) * 0.5


def along_lat(field_ext):
    return (field_ext[..., 2:, 1:-1] - field_ext[..., :-2, 1:-1]) * 0.5


def filter_block(work_block, block_cutoff):
    lon_parts = lax.axis_size("lon")
    components, levels, rows_here, width_here = work_block.shape
    planes = components * levels // lon_parts
    group = lon_parts // 4
    lines = work_block.reshape(lon_parts, planes, rows_here, width_here)
    circles = lax.all_to_all(lines, "lon", split_axis=0, concat_axis=0, tiled=True)
    quarters = circles.reshape(4, group, planes, rows_here, width_here)
    quarters = jnp.moveaxis(quarters, 1, 3).reshape(4, planes, rows_here, group * width_here)
    smoothed = damp_quarters(quarters, block_cutoff)
    smoothed = smoothed.reshape(4, planes, rows_here, group, width_here)
    smoothed = jnp.moveaxis(smoothed, 3, 1).reshape(lines.shape)
    returned = lax.all_to_all(smoothed, "lon", split_axis=0, concat_axis=0, tiled=True)
    return returned.reshape(work_block.shape)


def worker_group(band, bands):
    quarter = bands // 4
    low = band < bands // 2
    polar = jnp.logical_or(band < quarter, band >= bands - quarter)
    inner = jnp.where(low, band - quarter, band + quarter)
    source = jnp.where(polar, band, inner)
    helper = jnp.where(source < bands // 2, source + quarter, source - quarter)
    return polar, source, helper


def split_store(ref, values):
    rows, width = values.shape
    high = values.astype(jnp.bfloat16)
    low = (values - high.astype(jnp.float32)).astype(jnp.bfloat16)
    ref[:rows, :width] = high
    ref[rows:, :width] = low


def product(parts, high_ref, low_ref, out_ref, back):
    rows = out_ref.shape[0]
    dims = (((1,), (1 if back else 0,)), ((), ()))
    for start in range(0, out_ref.shape[1], 256):
        cols = slice(start, start + 256)
        piece = (cols, slice(None)) if back else (slice(None), cols)
        both = lax.dot_general(parts[...], high_ref[piece], dims, preferred_element_type=jnp.float32)
        cross = lax.dot_general(
            parts[:rows, :], low_ref[piece], dims, preferred_element_type=jnp.float32
        )
        out_ref[:, cols] = (both[:rows] + both[rows:]) + cross


def edge_tile(state, ring, courant, component, level, rows):
    rest = state.shape[3] % 128
    tail = state[component, level, rows, state.shape[3] - rest :]
    count = tail.shape[0]
    tail = jnp.concatenate([tail, jnp.zeros((count, 128 - rest), jnp.float32)], axis=1)
    lane = lax.broadcasted_iota(jnp.int32, (count, 128), 1)
    tile = jnp.where(lane == courant_lane, courant[rows, :], tail)
    tile = jnp.where((lane == rest) | (lane == rest + 1), ring[1, component, level, rows, :], tile)
    return jnp.where(lane >= 126, ring[0, component, level, rows, :], tile)


def substep_level(state, ring, caps, courant, field, work, level, first, last):
    components, levels, rows, quarter = state.shape
    width = field.shape[2]
    body = width - 128
    for c in range(components):
        field[c, 8 : 8 + rows, :body] = state[c, level, :, :body]
        field[c, 8 : 8 + rows, body:] = edge_tile(state, ring, courant, c, level, slice(0, rows))
        field[c, 6:8, :] = caps[0, 2 * (c * levels + level) : 2 * (c * levels + level) + 2, :]
        field[c, 8 + rows : 10 + rows, :] = caps[1, 2 * (c * levels + level) : 2 * (c * levels + level) + 2, :]
    east, north, theta, thick = (field[c] for c in range(4))
    height = east.shape[0]
    row_courant = east[:, body + courant_lane : body + courant_lane + 1]

    def along_x(f):
        return (pltpu.roll(f, width - 1, 1) - pltpu.roll(f, 1, 1)) * 0.5

    def along_y(f):
        return (pltpu.roll(f, height - 1, 0) - pltpu.roll(f, 1, 0)) * 0.5

    east_flux, north_flux = east * thick, north * thick
    new_thick = thick - row_courant * along_x(east_flux) - meridional_courant * along_y(north_flux)
    heat = (
        theta * thick
        - row_courant * along_x(east_flux * theta)
        - meridional_courant * along_y(north_flux * theta)
    )
    row = lax.broadcasted_iota(jnp.int32, (height, 1), 0)
    beyond = (first & (row < 8)) | (last & (row >= 8 + rows))
    heat = jnp.where(beyond, 0.0, heat)
    new_east = east - pressure_gain * row_courant * along_x(heat)
    new_north = north - pressure_gain * meridional_courant * along_y(heat)
    own = slice(8, 8 + rows)
    work[0, level] = new_east[own, :quarter]
    work[1, level] = new_north[own, :quarter]
    work[2, level] = heat[own, :quarter] / new_thick[own, :quarter]
    work[3, level] = new_thick[own, :quarter]


def circle_kernel(
    bands, parts, chunks, state, courant, gains, twists, table, out, circles, results, basis, high, low,
    operand, waves, pack, ring, edges, caps, field, work,
    send_sem, recv_sem, back_send_sem, back_recv_sem, local_sem, halo_send, halo_recv,
):
    part = lax.axis_index("lon")
    band = lax.axis_index("lat")
    polar, source, helper = worker_group(band, bands)
    _, _, per, rows, quarter = circles.shape
    components, levels, rows_here, _ = state.shape
    width = high.shape[1]
    lanes = width // 2
    row_chunks = rows_here // rows
    me = jnp.where(polar, part, part + parts)
    first, last = band == 0, band == bands - 1

    def block(ref, worker, chunk):
        level = (chunk // row_chunks) * 2 * per + (worker // parts) * per
        row = pl.multiple_of((chunk % row_chunks) * rows, rows)
        return ref.at[lax.rem(worker, parts), pl.ds(level, per), pl.ds(row, rows), :]

    load = pltpu.make_async_copy(table, basis, local_sem.at[0])
    load.start()

    caps[...] = jnp.zeros_like(caps)
    barrier = pltpu.get_barrier_semaphore()

    def greet(there, row_band):
        pl.semaphore_signal(barrier, inc=1, device_id=(there, row_band), device_id_type=MESH)

    for step in range(1, parts):
        greet(lax.rem(part + step, parts), band)
    for step in range(parts):
        greet(lax.rem(part + step, parts), jnp.where(polar, helper, source))

    @pl.when(band > 0)
    def _():
        greet(part, band - 1)

    @pl.when(band < bands - 1)
    def _():
        greet(part, band + 1)

    rest = quarter % 128
    lane = lax.broadcasted_iota(jnp.int32, (rows_here, 128), 1)

    @pl.loop(0, levels)
    def _(level):
        for c in range(components):
            begin = pltpu.roll(state[c, level, :, :128], rest, 1)
            tail = state[c, level, :, quarter - rest :]
            tail = jnp.concatenate([tail, jnp.zeros((rows_here, 128 - rest), jnp.float32)], axis=1)
            pack[c, level] = jnp.where(lane >= 126, pltpu.roll(tail, 128 - rest, 1), begin)

    inner_bands = jnp.where(first | last, 1, 2)
    pl.semaphore_wait(barrier, 2 * parts - 1 + inner_bands)
    columns = [
        pltpu.make_async_remote_copy(
            src_ref=pack,
            dst_ref=ring.at[slot],
            send_sem=halo_send.at[slot],
            recv_sem=halo_recv.at[slot],
            device_id=(lax.rem(part + shift, parts), band),
            device_id_type=MESH,
        )
        for slot, shift in ((0, 1), (1, parts - 1))
    ]
    for copy in columns:
        copy.start()
    field[...] = jnp.zeros_like(field)
    operand[...] = jnp.zeros_like(operand)
    load.wait()

    @pl.loop(0, width // 32)
    def _(step):
        at = pl.ds(pl.multiple_of(step * 32, 32), 32)
        exact = basis[at, :]
        upper = exact.astype(jnp.bfloat16)
        high[at, :] = upper
        low[at, :] = (exact - upper.astype(jnp.float32)).astype(jnp.bfloat16)

    for copy in columns:
        copy.wait()

    body = width - 128
    for c in range(components):
        for level in range(levels):
            at = slice(2 * (c * levels + level), 2 * (c * levels + level) + 2)
            for slot, own in ((0, slice(rows_here - 2, rows_here)), (1, slice(0, 2))):
                edges[slot, at, :body] = state[c, level, own, :body]
                edges[slot, at, body:] = edge_tile(state, ring, courant, c, level, own)

    def rows_to(slot, row_band):
        return pltpu.make_async_remote_copy(
            src_ref=edges.at[slot],
            dst_ref=caps.at[slot],
            send_sem=halo_send.at[2 + slot],
            recv_sem=halo_recv.at[2 + slot],
            device_id=(part, row_band),
            device_id_type=MESH,
        )

    @pl.when(jnp.logical_not(last))
    def _():
        rows_to(0, band + 1).start()

    @pl.when(jnp.logical_not(first))
    def _():
        rows_to(1, band - 1).start()

    @pl.when(jnp.logical_not(first))
    def _():
        rows_to(1, band - 1).wait_send()
        pltpu.make_async_copy(caps.at[0], caps.at[0], halo_recv.at[2]).wait()

    @pl.when(jnp.logical_not(last))
    def _():
        rows_to(0, band + 1).wait_send()
        pltpu.make_async_copy(caps.at[1], caps.at[1], halo_recv.at[3]).wait()

    through = pltpu.make_async_copy(work, out, local_sem.at[1])

    def send_chunk(chunk):
        for step in range(parts):
            there = lax.rem(part + step, parts)
            pltpu.make_async_remote_copy(
                src_ref=block(work, there + parts, chunk),
                dst_ref=circles.at[chunk, part],
                send_sem=send_sem.at[chunk, there + parts],
                recv_sem=recv_sem.at[chunk, part],
                device_id=(there, helper),
                device_id_type=MESH,
            ).start()
            if step == 0:
                pltpu.make_async_copy(
                    block(work, me, chunk), circles.at[chunk, part], recv_sem.at[chunk, part]
                ).start()
            else:
                pltpu.make_async_remote_copy(
                    src_ref=block(work, there, chunk),
                    dst_ref=circles.at[chunk, part],
                    send_sem=send_sem.at[chunk, there],
                    recv_sem=recv_sem.at[chunk, part],
                    device_id=(there, band),
                    device_id_type=MESH,
                ).start()

    span = 2 * per
    for begin in range(0, levels, span):
        for level in range(begin, begin + span):
            substep_level(state, ring, caps, courant, field, work, level, first, last)

        @pl.when(polar)
        def _():
            @pl.loop(begin // span * row_chunks, (begin // span + 1) * row_chunks)
            def _(chunk):
                send_chunk(chunk)

    @pl.when(jnp.logical_not(polar))
    def _():
        through.start()

    cos1, sin1, cos2, sin2 = (twists[i : i + 1, :] for i in range(4))
    half, whole = rows, per * rows

    @pl.loop(0, chunks)
    def _(chunk):
        for i in range(parts):
            slot = circles.at[chunk, i]
            pltpu.make_async_copy(slot, slot, recv_sem.at[chunk, i]).wait()
        q0, q1, q2, q3 = (circles[chunk, i].reshape(whole, quarter) for i in range(4))
        sum_a, sum_b, odd_a, odd_b = q0 + q2, q1 + q3, q0 - q2, q1 - q3
        skew = sum_a - sum_b
        skew_a, skew_b = skew[:half], skew[half:]
        stack = jnp.concatenate(
            [
                sum_a + sum_b,
                skew_a * cos2 + skew_b * sin2,
                skew_b * cos2 - skew_a * sin2,
                odd_a * cos1 - odd_b * sin1,
                -odd_a * sin1 - odd_b * cos1,
            ],
            axis=0,
        )
        split_store(operand, stack)
        product(operand, high, low, waves, False)
        row = pl.multiple_of((chunk % row_chunks) * rows, rows)
        g = [gains[i, pl.ds(row, rows), :] for i in range(5)]
        same0, same2, cross2, same1, cross1 = (
            g[0], g[1], g[2], jnp.concatenate([g[3]] * per), jnp.concatenate([g[4]] * per)
        )
        same0 = jnp.concatenate([same0] * per)
        cos_part, sin_part = waves[:, :lanes], waves[:, lanes:]
        two_a, two_b = slice(whole, whole + half), slice(whole + half, 2 * whole)
        one_a, one_b = slice(2 * whole, 3 * whole), slice(3 * whole, 4 * whole)
        rc2, rs2, ic2, is2 = mix(
            cos_part[two_a], sin_part[two_a], cos_part[two_b], sin_part[two_b], same2, cross2
        )
        rc1, rs1, ic1, is1 = mix(
            cos_part[one_a], sin_part[one_a], cos_part[one_b], sin_part[one_b], same1, cross1
        )
        damped = jnp.concatenate(
            [
                jnp.concatenate([same0 * cos_part[:whole], rc2, ic2, rc1, ic1], axis=0),
                jnp.concatenate([same0 * sin_part[:whole], rs2, is2, rs1, is1], axis=0),
            ],
            axis=1,
        )
        split_store(operand, damped)
        product(operand, high, low, waves, True)
        back = waves[:, :quarter]
        even, two_real, two_imag = back[:whole], back[two_a], back[two_b]
        one_real, one_imag = back[one_a], back[one_b]
        odd_a = one_real * cos1 - one_imag * sin1
        odd_b = -one_real * sin1 - one_imag * cos1
        skew = jnp.concatenate(
            [two_real * cos2 - two_imag * sin2, two_imag * cos2 + two_real * sin2], axis=0
        )
        plus, minus = even + skew, even - skew
        shape = (per, rows, quarter)
        results[chunk, 0] = (plus + odd_a).reshape(shape)
        results[chunk, 1] = (minus + odd_b).reshape(shape)
        results[chunk, 2] = (plus - odd_a).reshape(shape)
        results[chunk, 3] = (minus - odd_b).reshape(shape)
        if quarter < width:
            operand[:, quarter:] = jnp.zeros_like(operand[:, quarter:])
        for step in range(1, parts):
            there = lax.rem(part + step, parts)
            pltpu.make_async_remote_copy(
                src_ref=results.at[chunk, there],
                dst_ref=block(out, me, chunk),
                send_sem=back_send_sem.at[chunk, there],
                recv_sem=back_recv_sem.at[chunk, me],
                device_id=(there, source),
                device_id_type=MESH,
            ).start()

        @pl.when(polar)
        def _():
            pltpu.make_async_copy(
                results.at[chunk, part], block(out, me, chunk), back_recv_sem.at[chunk, me]
            ).start()

        @pl.when(jnp.logical_not(polar))
        def _():
            pltpu.make_async_remote_copy(
                src_ref=results.at[chunk, part],
                dst_ref=block(out, me, chunk),
                send_sem=back_send_sem.at[chunk, part],
                recv_sem=back_recv_sem.at[chunk, me],
                device_id=(part, source),
                device_id_type=MESH,
            ).start()

    def drain(ref, semaphore):
        pltpu.make_async_copy(ref, ref, semaphore).wait()

    @pl.loop(0, chunks)
    def _(chunk):
        for step in range(1, parts):
            there = lax.rem(part + step, parts)
            drain(results.at[chunk, there], back_send_sem.at[chunk, there])

        @pl.when(jnp.logical_not(polar))
        def _():
            drain(results.at[chunk, part], back_send_sem.at[chunk, part])

        @pl.when(polar)
        def _():
            for step in range(parts):
                there = lax.rem(part + step, parts)
                drain(block(work, there + parts, chunk), send_sem.at[chunk, there + parts])
                drain(block(out, there + parts, chunk), back_recv_sem.at[chunk, there + parts])
                drain(block(out, there, chunk), back_recv_sem.at[chunk, there])
                if step > 0:
                    drain(block(work, there, chunk), send_sem.at[chunk, there])

    @pl.when(jnp.logical_not(polar))
    def _():
        through.wait()


def shared_substep(state, courant, cutoff):
    parts, bands = lax.axis_size("lon"), lax.axis_size("lat")
    components, levels, rows_here, quarter = state.shape
    per, rows = 2, 32
    chunks = (components * levels // (2 * parts) // per) * (rows_here // rows)
    basis = quarter_basis(quarter)
    width = basis.shape[1]
    square = np.zeros((width, width), np.float32)
    square[:quarter] = basis
    cos_twist, sin_twist = quarter_twists(quarter)
    twists = jnp.asarray(np.stack([cos_twist[0], sin_twist[0], cos_twist[1], sin_twist[1]]))
    _, source, _ = worker_group(lax.axis_index("lat"), bands)
    row_cutoff = lax.dynamic_slice_in_dim(cutoff, source * rows_here, rows_here)
    same0, two, one = damping_tables(row_cutoff, quarter)
    gains = jnp.stack([same0, *two, *one])
    vmem, anywhere = pl.BlockSpec(memory_space=pltpu.VMEM), pl.BlockSpec(memory_space=pl.ANY)
    table = pltpu.VMEM((width, width), jnp.bfloat16)
    piece = pltpu.VMEM((chunks, parts, per, rows, quarter), jnp.float32)
    lines = 4 * per * rows
    pairs = 2 * components * levels
    return pl.pallas_call(
        functools.partial(circle_kernel, bands, parts, chunks),
        out_shape=jax.ShapeDtypeStruct(state.shape, jnp.float32),
        in_specs=[vmem, vmem, vmem, vmem, anywhere],
        out_specs=anywhere,
        scratch_shapes=[
            piece,
            piece,
            pltpu.VMEM((width, width), jnp.float32),
            table,
            table,
            pltpu.VMEM((2 * lines, width), jnp.bfloat16),
            pltpu.VMEM((lines, width), jnp.float32),
            pltpu.VMEM((components, levels, rows_here, 128), jnp.float32),
            pltpu.VMEM((2, components, levels, rows_here, 128), jnp.float32),
            pltpu.VMEM((2, pairs, width), jnp.float32),
            pltpu.VMEM((2, pairs, width), jnp.float32),
            pltpu.VMEM((components, rows_here + 16, width), jnp.float32),
            pltpu.VMEM(state.shape, jnp.float32),
            pltpu.SemaphoreType.DMA((chunks, 2 * parts)),
            pltpu.SemaphoreType.DMA((chunks, parts)),
            pltpu.SemaphoreType.DMA((chunks, parts)),
            pltpu.SemaphoreType.DMA((chunks, 2 * parts)),
            pltpu.SemaphoreType.DMA((2,)),
            pltpu.SemaphoreType.DMA((4,)),
            pltpu.SemaphoreType.DMA((4,)),
        ],
        compiler_params=pltpu.CompilerParams(
            collective_id=0, has_side_effects=True, vmem_limit_bytes=56 * 2**20
        ),
    )(state, courant[:, None], gains, twists, jnp.asarray(square))


def fits_shared(state):
    parts, bands = lax.axis_size("lon"), lax.axis_size("lat")
    components, levels, rows_here, quarter = state.shape
    return (
        parts == 4
        and components == parts
        and bands % 4 == 0
        and levels % 4 == 0
        and rows_here % 32 == 0
        and quarter % 128 == 32
    )


def per_device(model_state, courant, cutoff):
    if fits_shared(model_state):
        return shared_substep(model_state, courant, cutoff)
    rows_here = model_state.shape[2]
    band_index = lax.axis_index("lat")
    extended = with_halo(model_state, (("lon", 3), ("lat", 2)), 1)
    extended = trim_rims(extended, 2)
    wind_east = extended[0]
    wind_north = extended[1]
    theta_ext = extended[2]
    thickness = extended[3]
    row_courant = courant[None, :, None]
    east_flux = wind_east * thickness
    north_flux = wind_north * thickness
    heat_content = theta_ext * thickness
    new_thickness = (
        thickness[:, 1:-1, 1:-1]
        - row_courant * along_lon(east_flux)
        - meridional_courant * along_lat(north_flux)
    )
    new_heat = (
        heat_content[:, 1:-1, 1:-1]
        - row_courant * along_lon(east_flux * theta_ext)
        - meridional_courant * along_lat(north_flux * theta_ext)
    )
    new_theta = new_heat / new_thickness
    heat_ext = trim_rims(with_halo(new_heat, (("lon", 2), ("lat", 1)), 1), 1)
    new_east = wind_east[:, 1:-1, 1:-1] - pressure_gain * row_courant * along_lon(heat_ext)
    new_north = wind_north[:, 1:-1, 1:-1] - pressure_gain * meridional_courant * along_lat(heat_ext)
    stacked = jnp.stack([new_east, new_north, new_theta, new_thickness])
    own_cut = lax.dynamic_slice_in_dim(cutoff, band_index * rows_here, rows_here)
    return filter_block(stacked, own_cut)


def solution(mesh):
    placed = (P(None, None, "lat", "lon"), P("lat"), P())
    return jax.shard_map(
        per_device,
        mesh=mesh,
        in_specs=placed,
        out_specs=P(None, None, "lat", "lon"),
        check_vma=False,
    )
```

```python
import functools

import jax
import jax.numpy as jnp
import numpy as np
from jax import lax
from jax.experimental import pallas as pl
from jax.experimental.pallas import tpu as pltpu
from jax.sharding import PartitionSpec as P

meridional_courant = 0.05
pressure_gain = 4.0
courant_lane = 64
MESH = pl.DeviceIdType.MESH


def with_halo(array, sides, width):
    for axis, dim in sides:
        size, length = (lax.axis_size(axis), array.shape[dim])
        up = [(i, (i + 1) % size) for i in range(size)]
        down = [(j, i) for i, j in up]
        last = lax.slice_in_dim(array, length - width, length, axis=dim)
        first = lax.slice_in_dim(array, 0, width, axis=dim)
        before = lax.ppermute(last, axis, up)
        after = lax.ppermute(first, axis, down)
        array = jnp.concatenate([before, array, after], axis=dim)
    return array


def quarter_basis(quarter):
    half = quarter // 2
    lanes = -(-(half + 1) // 128) * 128
    phase = np.outer(np.arange(quarter), np.arange(half + 1)) % quarter
    angle = 2.0 * np.pi / quarter * phase
    table = np.zeros((quarter, 2 * lanes), np.float32)
    table[:, : half + 1] = np.cos(angle)
    table[:, lanes : lanes + half + 1] = np.sin(angle)
    return table


def quarter_twists(quarter):
    angle = 2.0 * np.pi / (4 * quarter) * np.outer([1.0, 2.0], np.arange(quarter))
    return np.cos(angle).astype(np.float32), np.sin(angle).astype(np.float32)


def damping_tables(row_cutoff, quarter):
    half = quarter // 2
    length = 4 * quarter
    lanes = -(-(half + 1) // 128) * 128
    index = jnp.arange(lanes, dtype=jnp.int32)
    inside = index <= half
    weight = jnp.where(inside, jnp.where((index == 0) | (index == half), 1.0, 2.0), 0.0) / quarter
    cut = row_cutoff.astype(jnp.float32)[:, None]

    def damping(wave_number):
        wave_number = jnp.abs(wave_number)
        folded = jnp.minimum(wave_number, length - wave_number)
        ratio = cut / jnp.maximum(folded, 1).astype(jnp.float32)[None, :]
        return jnp.minimum(1.0, ratio * ratio)

    def pair(shift, scale):
        above = damping(4 * index + shift)
        below = damping(4 * index - shift)
        gain = weight[None, :] * (0.5 * scale)
        return gain * (above + below), gain * (above - below)

    return pair(0, 0.25)[0], pair(2, 0.25), pair(1, 0.5)


def mix(real_cos, real_sin, imag_cos, imag_sin, same, cross):
    return (
        same * real_cos + cross * imag_sin,
        same * real_sin - cross * imag_cos,
        same * imag_cos - cross * real_sin,
        same * imag_sin + cross * real_cos,
    )


def damp_quarters(quarters, row_cutoff):
    _, planes, rows, quarter = quarters.shape
    basis = jnp.asarray(quarter_basis(quarter))
    cos_twist, sin_twist = quarter_twists(quarter)
    q0, q1, q2, q3 = quarters
    even, odd_a, odd_b = (q0 + q2) + (q1 + q3), q0 - q2, q1 - q3
    skew = (q0 + q2) - (q1 + q3)
    pairs = planes // 2
    skew_a, skew_b = skew[:pairs], skew[pairs:]
    one_real = odd_a * cos_twist[0] - odd_b * sin_twist[0]
    one_imag = -odd_a * sin_twist[0] - odd_b * cos_twist[0]
    two_real = skew_a * cos_twist[1] + skew_b * sin_twist[1]
    two_imag = skew_b * cos_twist[1] - skew_a * sin_twist[1]
    stack = jnp.concatenate([even, two_real, two_imag, one_real, one_imag], axis=0)
    waves = jnp.einsum("prm,mk->prk", stack, basis, precision=lax.Precision.HIGH)
    lanes = basis.shape[1] // 2
    cos_part, sin_part = waves[..., :lanes], waves[..., lanes:]
    same0, (same2, cross2), (same1, cross1) = damping_tables(row_cutoff, quarter)
    p, h = planes, pairs
    two = slice(p, p + h), slice(p + h, 2 * p)
    one = slice(2 * p, 3 * p), slice(3 * p, 4 * p)
    even_c, even_s = same0 * cos_part[:p], same0 * sin_part[:p]
    rc2, rs2, ic2, is2 = mix(
        cos_part[two[0]], sin_part[two[0]], cos_part[two[1]], sin_part[two[1]], same2, cross2
    )
    rc1, rs1, ic1, is1 = mix(
        cos_part[one[0]], sin_part[one[0]], cos_part[one[1]], sin_part[one[1]], same1, cross1
    )
    damped = jnp.concatenate(
        [
            jnp.concatenate([even_c, rc2, ic2, rc1, ic1], axis=0),
            jnp.concatenate([even_s, rs2, is2, rs1, is1], axis=0),
        ],
        axis=-1,
    )
    back = jnp.einsum("prk,mk->prm", damped, basis, precision=lax.Precision.HIGH)
    even, two_real, two_imag = back[:p], back[two[0]], back[two[1]]
    one_real, one_imag = back[one[0]], back[one[1]]
    odd_a = one_real * cos_twist[0] - one_imag * sin_twist[0]
    odd_b = -one_real * sin_twist[0] - one_imag * cos_twist[0]
    skew = jnp.concatenate(
        [
            two_real * cos_twist[1] - two_imag * sin_twist[1],
            two_imag * cos_twist[1] + two_real * sin_twist[1],
        ],
        axis=0,
    )
    plus, minus = even + skew, even - skew
    return jnp.stack([plus + odd_a, minus + odd_b, plus - odd_a, minus - odd_b])


def trim_rims(extended, row_dim):
    band_index = lax.axis_index("lat")
    band_count = lax.axis_size("lat")
    rows_ext = extended.shape[row_dim]
    positions = jnp.arange(rows_ext, dtype=jnp.int32)
    keep_rows = jnp.logical_not(
        (positions == 0) & (band_index == 0)
        | (positions == rows_ext - 1) & (band_index == band_count - 1)
    )
    mask_shape = [1] * extended.ndim
    mask_shape[row_dim] = rows_ext
    return extended * keep_rows.astype(extended.dtype).reshape(mask_shape)


def along_lon(field_ext):
    return (field_ext[..., 1:-1, 2:] - field_ext[..., 1:-1, :-2]) * 0.5


def along_lat(field_ext):
    return (field_ext[..., 2:, 1:-1] - field_ext[..., :-2, 1:-1]) * 0.5


def filter_block(work_block, block_cutoff):
    lon_parts = lax.axis_size("lon")
    components, levels, rows_here, width_here = work_block.shape
    planes = components * levels // lon_parts
    group = lon_parts // 4
    lines = work_block.reshape(lon_parts, planes, rows_here, width_here)
    circles = lax.all_to_all(lines, "lon", split_axis=0, concat_axis=0, tiled=True)
    quarters = circles.reshape(4, group, planes, rows_here, width_here)
    quarters = jnp.moveaxis(quarters, 1, 3).reshape(4, planes, rows_here, group * width_here)
    smoothed = damp_quarters(quarters, block_cutoff)
    smoothed = smoothed.reshape(4, planes, rows_here, group, width_here)
    smoothed = jnp.moveaxis(smoothed, 3, 1).reshape(lines.shape)
    returned = lax.all_to_all(smoothed, "lon", split_axis=0, concat_axis=0, tiled=True)
    return returned.reshape(work_block.shape)


def worker_group(band, bands):
    quarter = bands // 4
    low = band < bands // 2
    polar = jnp.logical_or(band < quarter, band >= bands - quarter)
    inner = jnp.where(low, band - quarter, band + quarter)
    source = jnp.where(polar, band, inner)
    helper = jnp.where(source < bands // 2, source + quarter, source - quarter)
    return polar, source, helper


def split_store(ref, values):
    rows, width = values.shape
    high = values.astype(jnp.bfloat16)
    low = (values - high.astype(jnp.float32)).astype(jnp.bfloat16)
    ref[:rows, :width] = high
    ref[rows:, :width] = low


def product(parts, high_ref, low_ref, out_ref, back):
    rows = out_ref.shape[0]
    dims = (((1,), (1 if back else 0,)), ((), ()))
    for start in range(0, out_ref.shape[1], 256):
        cols = slice(start, start + 256)
        piece = (cols, slice(None)) if back else (slice(None), cols)
        both = lax.dot_general(parts[...], high_ref[piece], dims, preferred_element_type=jnp.float32)
        cross = lax.dot_general(
            parts[:rows, :], low_ref[piece], dims, preferred_element_type=jnp.float32
        )
        out_ref[:, cols] = (both[:rows] + both[rows:]) + cross


def edge_tile(state, ring, courant, component, level, rows):
    rest = state.shape[3] % 128
    tail = state[component, level, rows, state.shape[3] - rest :]
    count = tail.shape[0]
    tail = jnp.concatenate([tail, jnp.zeros((count, 128 - rest), jnp.float32)], axis=1)
    lane = lax.broadcasted_iota(jnp.int32, (count, 128), 1)
    tile = jnp.where(lane == courant_lane, courant[rows, :], tail)
    tile = jnp.where((lane == rest) | (lane == rest + 1), ring[1, component, level, rows, :], tile)
    return jnp.where(lane >= 126, ring[0, component, level, rows, :], tile)


def substep_level(state, ring, caps, courant, field, work, level, first, last):
    components, levels, rows, quarter = state.shape
    width = field.shape[2]
    body = width - 128
    for c in range(components):
        field[c, 8 : 8 + rows, :body] = state[c, level, :, :body]
        field[c, 8 : 8 + rows, body:] = edge_tile(state, ring, courant, c, level, slice(0, rows))
        field[c, 6:8, :] = caps[0, 2 * (c * levels + level) : 2 * (c * levels + level) + 2, :]
        field[c, 8 + rows : 10 + rows, :] = caps[1, 2 * (c * levels + level) : 2 * (c * levels + level) + 2, :]
    east, north, theta, thick = (field[c] for c in range(4))
    height = east.shape[0]
    row_courant = east[:, body + courant_lane : body + courant_lane + 1]

    def along_x(f):
        return (pltpu.roll(f, width - 1, 1) - pltpu.roll(f, 1, 1)) * 0.5

    def along_y(f):
        return (pltpu.roll(f, height - 1, 0) - pltpu.roll(f, 1, 0)) * 0.5

    east_flux, north_flux = east * thick, north * thick
    new_thick = thick - row_courant * along_x(east_flux) - meridional_courant * along_y(north_flux)
    heat = (
        theta * thick
        - row_courant * along_x(east_flux * theta)
        - meridional_courant * along_y(north_flux * theta)
    )
    row = lax.broadcasted_iota(jnp.int32, (height, 1), 0)
    beyond = (first & (row < 8)) | (last & (row >= 8 + rows))
    heat = jnp.where(beyond, 0.0, heat)
    new_east = east - pressure_gain * row_courant * along_x(heat)
    new_north = north - pressure_gain * meridional_courant * along_y(heat)
    own = slice(8, 8 + rows)
    work[0, level] = new_east[own, :quarter]
    work[1, level] = new_north[own, :quarter]
    work[2, level] = heat[own, :quarter] / new_thick[own, :quarter]
    work[3, level] = new_thick[own, :quarter]


def circle_kernel(
    bands, parts, chunks, state, courant, gains, twists, table, out, circles, results, basis, high, low,
    operand, waves, pack, ring, edges, caps, field, work,
    send_sem, recv_sem, back_send_sem, back_recv_sem, local_sem, halo_send, halo_recv,
):
    part = lax.axis_index("lon")
    band = lax.axis_index("lat")
    polar, source, helper = worker_group(band, bands)
    _, _, per, rows, quarter = circles.shape
    components, levels, rows_here, _ = state.shape
    width = high.shape[1]
    lanes = width // 2
    row_chunks = rows_here // rows
    me = jnp.where(polar, part, part + parts)
    first, last = band == 0, band == bands - 1

    def block(ref, worker, chunk):
        level = (chunk // row_chunks) * 2 * per + (worker // parts) * per
        row = pl.multiple_of((chunk % row_chunks) * rows, rows)
        return ref.at[lax.rem(worker, parts), pl.ds(level, per), pl.ds(row, rows), :]

    load = pltpu.make_async_copy(table, basis, local_sem.at[0])
    load.start()

    caps[...] = jnp.zeros_like(caps)
    barrier = pltpu.get_barrier_semaphore()

    def greet(there, row_band):
        pl.semaphore_signal(barrier, inc=1, device_id=(there, row_band), device_id_type=MESH)

    for step in range(1, parts):
        greet(lax.rem(part + step, parts), band)
    for step in range(parts):
        greet(lax.rem(part + step, parts), jnp.where(polar, helper, source))

    @pl.when(band > 0)
    def _():
        greet(part, band - 1)

    @pl.when(band < bands - 1)
    def _():
        greet(part, band + 1)

    rest = quarter % 128
    lane = lax.broadcasted_iota(jnp.int32, (rows_here, 128), 1)

    @pl.loop(0, levels)
    def _(level):
        for c in range(components):
            begin = pltpu.roll(state[c, level, :, :128], rest, 1)
            tail = state[c, level, :, quarter - rest :]
            tail = jnp.concatenate([tail, jnp.zeros((rows_here, 128 - rest), jnp.float32)], axis=1)
            pack[c, level] = jnp.where(lane >= 126, pltpu.roll(tail, 128 - rest, 1), begin)

    inner_bands = jnp.where(first | last, 1, 2)
    pl.semaphore_wait(barrier, 2 * parts - 1 + inner_bands)
    columns = [
        pltpu.make_async_remote_copy(
            src_ref=pack,
            dst_ref=ring.at[slot],
            send_sem=halo_send.at[slot],
            recv_sem=halo_recv.at[slot],
            device_id=(lax.rem(part + shift, parts), band),
            device_id_type=MESH,
        )
        for slot, shift in ((0, 1), (1, parts - 1))
    ]
    for copy in columns:
        copy.start()
    field[...] = jnp.zeros_like(field)
    operand[...] = jnp.zeros_like(operand)
    load.wait()

    @pl.loop(0, width // 32)
    def _(step):
        at = pl.ds(pl.multiple_of(step * 32, 32), 32)
        exact = basis[at, :]
        upper = exact.astype(jnp.bfloat16)
        high[at, :] = upper
        low[at, :] = (exact - upper.astype(jnp.float32)).astype(jnp.bfloat16)

    for copy in columns:
        copy.wait()

    body = width - 128
    for c in range(components):
        for level in range(levels):
            at = slice(2 * (c * levels + level), 2 * (c * levels + level) + 2)
            for slot, own in ((0, slice(rows_here - 2, rows_here)), (1, slice(0, 2))):
                edges[slot, at, :body] = state[c, level, own, :body]
                edges[slot, at, body:] = edge_tile(state, ring, courant, c, level, own)

    def rows_to(slot, row_band):
        return pltpu.make_async_remote_copy(
            src_ref=edges.at[slot],
            dst_ref=caps.at[slot],
            send_sem=halo_send.at[2 + slot],
            recv_sem=halo_recv.at[2 + slot],
            device_id=(part, row_band),
            device_id_type=MESH,
        )

    @pl.when(jnp.logical_not(last))
    def _():
        rows_to(0, band + 1).start()

    @pl.when(jnp.logical_not(first))
    def _():
        rows_to(1, band - 1).start()

    @pl.when(jnp.logical_not(first))
    def _():
        rows_to(1, band - 1).wait_send()
        pltpu.make_async_copy(caps.at[0], caps.at[0], halo_recv.at[2]).wait()

    @pl.when(jnp.logical_not(last))
    def _():
        rows_to(0, band + 1).wait_send()
        pltpu.make_async_copy(caps.at[1], caps.at[1], halo_recv.at[3]).wait()

    through = pltpu.make_async_copy(work, out, local_sem.at[1])

    def send_chunk(chunk):
        for step in range(parts):
            there = lax.rem(part + step, parts)
            pltpu.make_async_remote_copy(
                src_ref=block(work, there + parts, chunk),
                dst_ref=circles.at[chunk, part],
                send_sem=send_sem.at[chunk, there + parts],
                recv_sem=recv_sem.at[chunk, part],
                device_id=(there, helper),
                device_id_type=MESH,
            ).start()
            if step == 0:
                pltpu.make_async_copy(
                    block(work, me, chunk), circles.at[chunk, part], recv_sem.at[chunk, part]
                ).start()
            else:
                pltpu.make_async_remote_copy(
                    src_ref=block(work, there, chunk),
                    dst_ref=circles.at[chunk, part],
                    send_sem=send_sem.at[chunk, there],
                    recv_sem=recv_sem.at[chunk, part],
                    device_id=(there, band),
                    device_id_type=MESH,
                ).start()

    span = 2 * per
    for begin in range(0, levels, span):
        for level in range(begin, begin + span):
            substep_level(state, ring, caps, courant, field, work, level, first, last)

        @pl.when(polar)
        def _():
            @pl.loop(begin // span * row_chunks, (begin // span + 1) * row_chunks)
            def _(chunk):
                send_chunk(chunk)

    @pl.when(jnp.logical_not(polar))
    def _():
        through.start()

    cos1, sin1, cos2, sin2 = (twists[i : i + 1, :] for i in range(4))
    half, whole = rows, per * rows

    @pl.loop(0, chunks)
    def _(chunk):
        for i in range(parts):
            slot = circles.at[chunk, i]
            pltpu.make_async_copy(slot, slot, recv_sem.at[chunk, i]).wait()
        q0, q1, q2, q3 = (circles[chunk, i].reshape(whole, quarter) for i in range(4))
        sum_a, sum_b, odd_a, odd_b = q0 + q2, q1 + q3, q0 - q2, q1 - q3
        skew = sum_a - sum_b
        skew_a, skew_b = skew[:half], skew[half:]
        stack = jnp.concatenate(
            [
                sum_a + sum_b,
                skew_a * cos2 + skew_b * sin2,
                skew_b * cos2 - skew_a * sin2,
                odd_a * cos1 - odd_b * sin1,
                -odd_a * sin1 - odd_b * cos1,
            ],
            axis=0,
        )
        split_store(operand, stack)
        product(operand, high, low, waves, False)
        row = pl.multiple_of((chunk % row_chunks) * rows, rows)
        g = [gains[i, pl.ds(row, rows), :] for i in range(5)]
        same0, same2, cross2, same1, cross1 = (
            g[0], g[1], g[2], jnp.concatenate([g[3]] * per), jnp.concatenate([g[4]] * per)
        )
        same0 = jnp.concatenate([same0] * per)
        cos_part, sin_part = waves[:, :lanes], waves[:, lanes:]
        two_a, two_b = slice(whole, whole + half), slice(whole + half, 2 * whole)
        one_a, one_b = slice(2 * whole, 3 * whole), slice(3 * whole, 4 * whole)
        rc2, rs2, ic2, is2 = mix(
            cos_part[two_a], sin_part[two_a], cos_part[two_b], sin_part[two_b], same2, cross2
        )
        rc1, rs1, ic1, is1 = mix(
            cos_part[one_a], sin_part[one_a], cos_part[one_b], sin_part[one_b], same1, cross1
        )
        damped = jnp.concatenate(
            [
                jnp.concatenate([same0 * cos_part[:whole], rc2, ic2, rc1, ic1], axis=0),
                jnp.concatenate([same0 * sin_part[:whole], rs2, is2, rs1, is1], axis=0),
            ],
            axis=1,
        )
        split_store(operand, damped)
        product(operand, high, low, waves, True)
        back = waves[:, :quarter]
        even, two_real, two_imag = back[:whole], back[two_a], back[two_b]
        one_real, one_imag = back[one_a], back[one_b]
        odd_a = one_real * cos1 - one_imag * sin1
        odd_b = -one_real * sin1 - one_imag * cos1
        skew = jnp.concatenate(
            [two_real * cos2 - two_imag * sin2, two_imag * cos2 + two_real * sin2], axis=0
        )
        plus, minus = even + skew, even - skew
        shape = (per, rows, quarter)
        results[chunk, 0] = (plus + odd_a).reshape(shape)
        results[chunk, 1] = (minus + odd_b).reshape(shape)
        results[chunk, 2] = (plus - odd_a).reshape(shape)
        results[chunk, 3] = (minus - odd_b).reshape(shape)
        if quarter < width:
            operand[:, quarter:] = jnp.zeros_like(operand[:, quarter:])
        for step in range(1, parts):
            there = lax.rem(part + step, parts)
            pltpu.make_async_remote_copy(
                src_ref=results.at[chunk, there],
                dst_ref=block(out, me, chunk),
                send_sem=back_send_sem.at[chunk, there],
                recv_sem=back_recv_sem.at[chunk, me],
                device_id=(there, source),
                device_id_type=MESH,
            ).start()

        @pl.when(polar)
        def _():
            pltpu.make_async_copy(
                results.at[chunk, part], block(out, me, chunk), back_recv_sem.at[chunk, me]
            ).start()

        @pl.when(jnp.logical_not(polar))
        def _():
            pltpu.make_async_remote_copy(
                src_ref=results.at[chunk, part],
                dst_ref=block(out, me, chunk),
                send_sem=back_send_sem.at[chunk, part],
                recv_sem=back_recv_sem.at[chunk, me],
                device_id=(part, source),
                device_id_type=MESH,
            ).start()

    def drain(ref, semaphore):
        pltpu.make_async_copy(ref, ref, semaphore).wait()

    @pl.loop(0, chunks)
    def _(chunk):
        for step in range(1, parts):
            there = lax.rem(part + step, parts)
            drain(results.at[chunk, there], back_send_sem.at[chunk, there])

        @pl.when(jnp.logical_not(polar))
        def _():
            drain(results.at[chunk, part], back_send_sem.at[chunk, part])

        @pl.when(polar)
        def _():
            for step in range(parts):
                there = lax.rem(part + step, parts)
                drain(block(work, there + parts, chunk), send_sem.at[chunk, there + parts])
                drain(block(out, there + parts, chunk), back_recv_sem.at[chunk, there + parts])
                drain(block(out, there, chunk), back_recv_sem.at[chunk, there])
                if step > 0:
                    drain(block(work, there, chunk), send_sem.at[chunk, there])

    @pl.when(jnp.logical_not(polar))
    def _():
        through.wait()


def shared_substep(state, courant, cutoff):
    parts, bands = lax.axis_size("lon"), lax.axis_size("lat")
    components, levels, rows_here, quarter = state.shape
    per, rows = 2, 8
    chunks = (components * levels // (2 * parts) // per) * (rows_here // rows)
    basis = quarter_basis(quarter)
    width = basis.shape[1]
    square = np.zeros((width, width), np.float32)
    square[:quarter] = basis
    cos_twist, sin_twist = quarter_twists(quarter)
    twists = jnp.asarray(np.stack([cos_twist[0], sin_twist[0], cos_twist[1], sin_twist[1]]))
    _, source, _ = worker_group(lax.axis_index("lat"), bands)
    row_cutoff = lax.dynamic_slice_in_dim(cutoff, source * rows_here, rows_here)
    same0, two, one = damping_tables(row_cutoff, quarter)
    gains = jnp.stack([same0, *two, *one])
    vmem, anywhere = pl.BlockSpec(memory_space=pltpu.VMEM), pl.BlockSpec(memory_space=pl.ANY)
    table = pltpu.VMEM((width, width), jnp.bfloat16)
    piece = pltpu.VMEM((chunks, parts, per, rows, quarter), jnp.float32)
    lines = 4 * per * rows
    pairs = 2 * components * levels
    return pl.pallas_call(
        functools.partial(circle_kernel, bands, parts, chunks),
        out_shape=jax.ShapeDtypeStruct(state.shape, jnp.float32),
        in_specs=[vmem, vmem, vmem, vmem, anywhere],
        out_specs=anywhere,
        scratch_shapes=[
            piece,
            piece,
            pltpu.VMEM((width, width), jnp.float32),
            table,
            table,
            pltpu.VMEM((2 * lines, width), jnp.bfloat16),
            pltpu.VMEM((lines, width), jnp.float32),
            pltpu.VMEM((components, levels, rows_here, 128), jnp.float32),
            pltpu.VMEM((2, components, levels, rows_here, 128), jnp.float32),
            pltpu.VMEM((2, pairs, width), jnp.float32),
            pltpu.VMEM((2, pairs, width), jnp.float32),
            pltpu.VMEM((components, rows_here + 16, width), jnp.float32),
            pltpu.VMEM(state.shape, jnp.float32),
            pltpu.SemaphoreType.DMA((chunks, 2 * parts)),
            pltpu.SemaphoreType.DMA((chunks, parts)),
            pltpu.SemaphoreType.DMA((chunks, parts)),
            pltpu.SemaphoreType.DMA((chunks, 2 * parts)),
            pltpu.SemaphoreType.DMA((2,)),
            pltpu.SemaphoreType.DMA((4,)),
            pltpu.SemaphoreType.DMA((4,)),
        ],
        compiler_params=pltpu.CompilerParams(
            collective_id=0, has_side_effects=True, vmem_limit_bytes=56 * 2**20
        ),
    )(state, courant[:, None], gains, twists, jnp.asarray(square))


def fits_shared(state):
    parts, bands = lax.axis_size("lon"), lax.axis_size("lat")
    components, levels, rows_here, quarter = state.shape
    return (
        parts == 4
        and components == parts
        and bands % 4 == 0
        and levels % 4 == 0
        and rows_here % 8 == 0
        and quarter % 128 == 32
    )


def per_device(model_state, courant, cutoff):
    if fits_shared(model_state):
        return shared_substep(model_state, courant, cutoff)
    rows_here = model_state.shape[2]
    band_index = lax.axis_index("lat")
    extended = with_halo(model_state, (("lon", 3), ("lat", 2)), 1)
    extended = trim_rims(extended, 2)
    wind_east = extended[0]
    wind_north = extended[1]
    theta_ext = extended[2]
    thickness = extended[3]
    row_courant = courant[None, :, None]
    east_flux = wind_east * thickness
    north_flux = wind_north * thickness
    heat_content = theta_ext * thickness
    new_thickness = (
        thickness[:, 1:-1, 1:-1]
        - row_courant * along_lon(east_flux)
        - meridional_courant * along_lat(north_flux)
    )
    new_heat = (
        heat_content[:, 1:-1, 1:-1]
        - row_courant * along_lon(east_flux * theta_ext)
        - meridional_courant * along_lat(north_flux * theta_ext)
    )
    new_theta = new_heat / new_thickness
    heat_ext = trim_rims(with_halo(new_heat, (("lon", 2), ("lat", 1)), 1), 1)
    new_east = wind_east[:, 1:-1, 1:-1] - pressure_gain * row_courant * along_lon(heat_ext)
    new_north = wind_north[:, 1:-1, 1:-1] - pressure_gain * meridional_courant * along_lat(heat_ext)
    stacked = jnp.stack([new_east, new_north, new_theta, new_thickness])
    own_cut = lax.dynamic_slice_in_dim(cutoff, band_index * rows_here, rows_here)
    return filter_block(stacked, own_cut)


def solution(mesh):
    placed = (P(None, None, "lat", "lon"), P("lat"), P())
    return jax.shard_map(
        per_device,
        mesh=mesh,
        in_specs=placed,
        out_specs=P(None, None, "lat", "lon"),
        check_vma=False,
    )
```
